32 devices in a mesh: proof: 8 (over y, x, core), landmark: 4 (over z).
Axes of the slice: x: 2, y: 2, z: 4, core: 2. Of those that a mesh axis runs over, the one named last changes fastest.
Arguments:
- row_features: bfloat16 [3072, 7168], P('proof', 'landmark'), may hold values from -48 to 48
- landmark_features: bfloat16 [2048, 7168], P('landmark', 'proof'), may hold values from -48 to 48
- targets: float32 [3072, 64], P('proof'), may hold values from -6 to 6
Outputs:
- coefficient: float32 [2048, 64], P('landmark')
- residual: float32 [2048, 64], P('landmark')
The draws below stay inside these ranges and needn't reach their ends.
All inputs are finite; a program needn't handle non-finite values.
Results may differ from the reference program's by a relative error of at most 0.0007.
Values may be sent and summed in bfloat16 or wider, within the bound.
No kernel may reach another device: no remote copies, remote signals or barrier semaphores. Data moves between devices by JAX's collectives and lax.ppermute only.
A program may use at most 64 MiB of HBM per device.

```python
import jax
import jax.numpy as jnp
from jax import lax

D = 7168
ROWS_DEV = 384
TARGETS = 64
ITERS = 2
SIGNAL = 32
SPREAD = 10690
NW = 3072
M = 2048


def column_scale():
    columns = jnp.arange(D)
    return jnp.where(columns < SIGNAL, 3.0, 1.0).astype(jnp.float32)


def shared_parts(key):
    table_key = jax.random.fold_in(key, 0)
    tables = 0.6 * jnp.clip(jax.random.normal(table_key, (3, 8, D), jnp.float32), -4.0, 4.0)
    return tables


def labelled_centres(label_key, tables, count):
    labels = jax.random.randint(label_key, (count, 3), 0, 8)
    centre = tables[0][labels[:, 0]] + tables[1][labels[:, 1]]
    return centre + tables[2][labels[:, 2]]


def draw_row_features(key, part):
    tables = shared_parts(key)
    key = jax.random.fold_in(key, 11)
    label_key, noise_key = jax.random.split(key)
    centre = labelled_centres(label_key, tables, NW)
    noise = 0.6 * jnp.clip(jax.random.normal(noise_key, (NW, D), jnp.float32), -4.0, 4.0)
    return ((centre + noise) * column_scale()[None, :]).astype(jnp.bfloat16)


def draw_landmark_features(key, part):
    tables = shared_parts(key)
    key = jax.random.fold_in(key, 23)
    label_key, noise_key = jax.random.split(key)
    centre = labelled_centres(label_key, tables, M)
    noise = 0.6 * jnp.clip(jax.random.normal(noise_key, (M, D), jnp.float32), -4.0, 4.0)
    return ((centre + noise) * column_scale()[None, :]).astype(jnp.bfloat16)


def levels(stream_key, dims, cuts, smallest, top_value):
    def one(dim, blocks):
        heights = jax.random.uniform(jax.random.fold_in(jax.random.fold_in(stream_key, 6), dim), (blocks,), jnp.float32, smallest / len(cuts), top_value / len(cuts))
        return jnp.repeat(jnp.exp(heights), dims[dim] // blocks).reshape((-1,) + (1,) * (len(dims) - dim - 1))

    gain = one(*cuts[0])
    for cut in cuts[1:]:
        gain = gain * one(*cut)
    return gain


def scatter_about(key, dims, spread, bound, cuts=(), dtype=jnp.bfloat16):
    array = jax.random.normal(key, dims, jnp.float32) * spread
    if len(cuts) > 0:
        array = levels(key, dims, cuts, -0.22, 0.18) * array
    return jnp.clip(array, min=-bound, max=bound).astype(dtype)


def setup_inputs(seed: int = 0) -> dict:
    arg_keys = jax.random.split(jax.random.key(seed), 4)
    row_features = draw_row_features(jax.random.fold_in(arg_keys[3], 71), 0)
    landmark_features = draw_landmark_features(jax.random.fold_in(arg_keys[3], 71), 0)
    targets = scatter_about(arg_keys[2], (NW, TARGETS), 1.0, 6.0, ((0, 8),), jnp.float32)
    return dict(row_features=row_features, landmark_features=landmark_features, targets=targets)


ridge_scale = 0.002


def kernel_rows(block, landmark_features, landmark_norm):
    cross = jnp.dot(block, landmark_features.T, preferred_element_type=jnp.float32)
    row_norm = jnp.sum(jnp.square(block.astype(jnp.float32)), axis=1)
    return jnp.exp(-(row_norm[:, None] + landmark_norm[None, :] - 2.0 * cross) / SPREAD)


def reference(row_features, landmark_features, targets):
    landmark_norm = jnp.sum(jnp.square(landmark_features.astype(jnp.float32)), axis=1)
    blocks = row_features.reshape(NW // ROWS_DEV, ROWS_DEV, D)
    kernel = lax.map(lambda block: kernel_rows(block, landmark_features, landmark_norm), blocks)
    kernel = kernel.reshape(NW, M)
    highest = lax.Precision.HIGHEST
    lam = ridge_scale * NW
    projected = jnp.dot(kernel.T, targets, precision=highest)
    precond = lam + jnp.sum(kernel * kernel, axis=0)
    coefficient = jnp.zeros_like(projected)
    residual = projected
    scaled = residual / precond[:, None]
    direction = scaled
    inner = jnp.sum(residual * scaled, axis=0)
    for iteration in range(ITERS):
        image = jnp.dot(kernel, direction, precision=highest)
        gradient = jnp.dot(kernel.T, image, precision=highest) + lam * direction
        curvature = jnp.sum(direction * gradient, axis=0)
        step_size = inner / curvature
        coefficient = coefficient + step_size * direction
        residual = residual - step_size * gradient
        scaled = residual / precond[:, None]
        inner_next = jnp.sum(residual * scaled, axis=0)
        direction = scaled + (inner_next / inner) * direction
        inner = inner_next
    return coefficient, residual
```

```python
import jax
import jax.numpy as jnp
from jax import lax
from jax.sharding import PartitionSpec as P

ITERS = 2
SPREAD = 10690

ridge_scale = 0.002


def squares(block):
    return jnp.sum(jnp.square(block.astype(jnp.float32)), axis=1)


def cross_piece(left, right):
    return lax.dot_general(
        left, right, (((1,), (1,)), ((), ())), preferred_element_type=jnp.float32
    )


def times(left, right, contract):
    return lax.dot_general(
        left, right, ((contract[:1], contract[1:]), ((), ())), precision=lax.Precision.HIGHEST
    )


def flipped(block, axis, bits):
    size = lax.axis_size(axis)
    return lax.ppermute(block, axis, [(i, i ^ bits) for i in range(size)])


def sum_rows_axis(block):
    size = lax.axis_size("proof")
    if size != 8:
        return lax.psum(block, "proof")
    odd = lax.axis_index("proof") % 2
    half = block.shape[1] // 2
    low, high = block[:, :half], block[:, half:]
    mine, other = jnp.where(odd == 0, low, high), jnp.where(odd == 0, high, low)
    mine = mine + flipped(other, "proof", 1)
    mine = mine + flipped(mine, "proof", 2) + flipped(mine, "proof", 4) + flipped(mine, "proof", 6)
    other = flipped(mine, "proof", 1)
    low, high = jnp.where(odd == 0, mine, other), jnp.where(odd == 0, other, mine)
    return jnp.concatenate([low, high], axis=1)


def sum_landmark_axis(block):
    size = lax.axis_size("landmark")
    if size != 4:
        return lax.psum(block, "landmark")
    total = block
    for shift in range(1, size):
        pairs = [(i, (i + shift) % size) for i in range(size)]
        total = total + lax.ppermute(block, "landmark", pairs)
    return total


def packed(block, *vectors):
    rows = jnp.stack(vectors)
    rows = jnp.pad(rows, ((0, 8 - rows.shape[0]), (0, block.shape[1] - rows.shape[1])))
    return jnp.concatenate([block, rows], axis=0)


def gathered_landmarks(piece):
    size = lax.axis_size("proof")
    if size != 8:
        return lax.all_gather(piece, "proof", axis=1, tiled=True)
    me = lax.axis_index("proof")
    half = piece.shape[0] // 2
    pieces = {0: piece, 2: flipped(piece, "proof", 2), 4: flipped(piece, "proof", 4)}
    corner_low = flipped(pieces[2][:half], "proof", 4)
    corner_high = flipped(pieces[4][half:], "proof", 2)
    pieces[6] = jnp.concatenate([corner_low, corner_high], axis=0)
    for bits in (0, 2, 4, 6):
        pieces[bits + 1] = flipped(pieces[bits], "proof", 1)
    whole = jnp.zeros((piece.shape[0], piece.shape[1] * size), piece.dtype)
    for bits, part in pieces.items():
        whole = lax.dynamic_update_slice(whole, part, (0, (me ^ bits) * piece.shape[1]))
    return whole


def squared_distances(row_features, landmark_features):
    size = lax.axis_size("landmark")
    me = lax.axis_index("landmark")
    width = row_features.shape[1]
    whole = gathered_landmarks(landmark_features)
    landmark_norm = squares(whole)

    def term(block, owner):
        start = jnp.clip(owner, 0, size - 1) * width
        other = lax.dynamic_slice_in_dim(whole, start, width, axis=1)
        return cross_piece(block, other)

    if size != 4:
        rows = lax.all_gather(row_features, "landmark", axis=1, tiled=True)
        return squares(rows)[:, None] + landmark_norm[None, :] - 2.0 * cross_piece(rows, whole)
    cross = term(row_features, me)
    row_norm = squares(row_features)
    up = [(i, i + 1) for i in range(size - 1)]
    down = [(i + 1, i) for i in range(size - 1)]
    below = above = row_features
    for step in range(1, size):
        below, above = lax.ppermute(below, "landmark", up), lax.ppermute(above, "landmark", down)
        cross = cross + term(below, me - step) + term(above, me + step)
        row_norm = row_norm + squares(below) + squares(above)
    return row_norm[:, None] + landmark_norm[None, :] - 2.0 * cross


def shards(row_features, landmark_features, targets):
    kernel = jnp.exp(-squared_distances(row_features, landmark_features) / SPREAD)
    lam = ridge_scale * row_features.shape[0] * lax.axis_size("proof")
    count = targets.shape[1]
    columns = targets.T
    sums = sum_rows_axis(packed(times(columns, kernel, (1, 0)), jnp.sum(kernel * kernel, axis=0)))
    residual, precond = sums[:count], lam + sums[count]
    coefficient = jnp.zeros_like(residual)
    inner = None
    for iteration in range(ITERS):
        scaled = residual / precond
        part = times(scaled, kernel, (1, 1))
        dots = [jnp.sum(residual * scaled, axis=1), jnp.sum(scaled * scaled, axis=1)]
        if iteration > 0:
            dots.append(jnp.sum(scaled * direction, axis=1))
        sums = sum_landmark_axis(packed(part, *dots))
        inner_next, square = sums[count, :count], sums[count + 1, :count]
        if iteration == 0:
            direction, image, length = scaled, sums[:count], square
        else:
            beta = inner_next / inner
            length = square + beta * (2.0 * sums[count + 2, :count] + beta * length)
            direction = scaled + beta[:, None] * direction
            image = sums[:count] + beta[:, None] * image
        inner = inner_next
        sums = sum_rows_axis(packed(times(image, kernel, (1, 0)), jnp.sum(image * image, axis=1)))
        gradient = sums[:count] + lam * direction
        step_size = (inner / (sums[count, :count] + lam * length))[:, None]
        coefficient = coefficient + step_size * direction
        residual = residual - step_size * gradient
    return coefficient.T, residual.T


def solution(mesh):
    placed = (P("proof", "landmark"), P("landmark", "proof"), P("proof", None))
    return jax.shard_map(
        shards,
        mesh=mesh,
        in_specs=placed,
        out_specs=(P("landmark", None), P("landmark", None)),
        check_vma=False,
    )
```

```python
import jax
import jax.numpy as jnp
from jax import lax
from jax.experimental import pallas as pl
from jax.experimental.pallas import tpu as pltpu
from jax.sharding import PartitionSpec as P

ITERS = 2
SPREAD = 10690

ridge_scale = 0.002


def squares(block):
    return jnp.sum(jnp.square(block.astype(jnp.float32)), axis=1)


def cross_piece(left, right):
    return lax.dot_general(
        left, right, (((1,), (1,)), ((), ())), preferred_element_type=jnp.float32
    )


def times(left, right, contract):
    return lax.dot_general(
        left, right, ((contract[:1], contract[1:]), ((), ())), precision=lax.Precision.HIGHEST
    )


TO_MIDDLE = [(0, 1), (3, 2)]
ACROSS = [(1, 2), (2, 1)]
TO_END = [(1, 0), (2, 3)]


def flipped(block, bits):
    return lax.ppermute(block, "proof", [(i, i ^ bits) for i in range(8)])


def sum_rows_axis(block):
    odd = lax.axis_index("proof") % 2
    half = block.shape[1] // 2
    low, high = block[:, :half], block[:, half:]
    mine, other = jnp.where(odd == 0, low, high), jnp.where(odd == 0, high, low)
    mine = mine + flipped(other, 1)
    mine = mine + flipped(mine, 2) + flipped(mine, 4) + flipped(mine, 6)
    other = flipped(mine, 1)
    low, high = jnp.where(odd == 0, mine, other), jnp.where(odd == 0, other, mine)
    return jnp.concatenate([low, high], axis=1)


def sum_middle(block):
    return block + lax.ppermute(block, "landmark", ACROSS)


def packed(block, *vectors):
    rows = jnp.stack(vectors)
    rows = jnp.pad(rows, ((0, 8 - rows.shape[0]), (0, block.shape[1] - rows.shape[1])))
    return jnp.concatenate([block, rows], axis=0)


def plane_pieces(piece):
    half = piece.shape[0] // 2
    across_x, across_y = flipped(piece, 2), flipped(piece, 4)
    corner_low, corner_high = flipped(across_x[:half], 4), flipped(across_y[half:], 2)
    found = [(0, 0, piece), (2, 0, across_x), (4, 0, across_y), (6, 0, corner_low), (6, half, corner_high)]
    return found + [(bits + 1, row, flipped(block, 1)) for bits, row, block in found]


def kernel_block(rows, landmarks, columns):
    n, count = columns.shape[1], columns.shape[0]
    m = max(row + block.shape[0] for _, row, block in landmarks)
    width = rows[0][2].shape[1]
    part = landmarks[0][2].shape[1]
    tile = 256
    place = jnp.stack([lax.axis_index("proof"), lax.axis_index("landmark")]).astype(jnp.int32)

    def body(place_ref, columns_ref, *refs):
        row_refs, landmark_refs = refs[: len(rows)], refs[len(rows) : len(rows) + len(landmarks)]
        kernel_ref, sums_ref, rows_s, land_s, cross_s, norm_s, row_sem, land_sem = refs[len(rows) + len(landmarks) :]
        p, z = place_ref[0], place_ref[1]
        for (bits, row, block), ref in zip(rows, row_refs):
            slot = z ^ bits
            pltpu.make_async_copy(ref, rows_s.at[slot, pl.ds(row, block.shape[0])], row_sem.at[slot]).start()
        for (bits, row, block), ref in zip(landmarks, landmark_refs):
            f = p ^ bits
            lane = pl.multiple_of((f % 2) * part, 128)
            target = land_s.at[f // 2, pl.ds(row, block.shape[0]), pl.ds(lane, part)]
            pltpu.make_async_copy(ref, target, land_sem.at[f // 2]).start()
        cross_s[...] = jnp.zeros_like(cross_s)
        norm_s[...] = jnp.zeros_like(norm_s)
        row_norm = jnp.zeros((n, 128), jnp.float32)
        for b in range(4):
            pltpu.make_async_copy(rows_s.at[b], rows_s.at[b], row_sem.at[b]).wait()
            pltpu.make_async_copy(land_s.at[b], land_s.at[b], land_sem.at[b]).wait()
            for j in range(width // 128):
                x = rows_s[b, :, j * 128 : (j + 1) * 128].astype(jnp.float32)
                row_norm = row_norm + x * x

            @pl.loop(0, m // tile)
            def _(t):
                start = pl.multiple_of(t * tile, tile)
                cross_s[t] += lax.dot_general(
                    rows_s[b], land_s[b, pl.ds(start, tile)], (((1,), (1,)), ((), ())),
                    preferred_element_type=jnp.float32,
                )
                total = norm_s[pl.ds(start, tile)]
                for j in range(width // 128):
                    x = land_s[b, pl.ds(start, tile), j * 128 : (j + 1) * 128].astype(jnp.float32)
                    total = total + x * x
                norm_s[pl.ds(start, tile)] = total

        row_norm = jnp.sum(row_norm, axis=1, keepdims=True)
        for t in range(m // tile):
            inside = slice(t * tile, (t + 1) * tile)
            landmark_norm = lax.dot_general(
                jnp.ones((8, 128), jnp.float32), norm_s[inside], (((1,), (1,)), ((), ())),
                precision=lax.Precision.HIGHEST,
            )[:1]
            k = jnp.exp(-(row_norm + landmark_norm - 2.0 * cross_s[t]) / SPREAD)
            kernel_ref[:, inside] = k
            sums_ref[:count, inside] = jnp.dot(columns_ref[...], k, precision=lax.Precision.HIGHEST)
            sums_ref[count:, inside] = jnp.broadcast_to(jnp.sum(k * k, axis=0, keepdims=True), (8, tile))

    any_spec = pl.BlockSpec(memory_space=pl.ANY)
    vmem = pl.BlockSpec(memory_space=pltpu.VMEM)
    blocks = [block for _, _, block in rows] + [block for _, _, block in landmarks]
    return pl.pallas_call(
        body,
        out_shape=(
            jax.ShapeDtypeStruct((n, m), jnp.float32),
            jax.ShapeDtypeStruct((count + 8, m), jnp.float32),
        ),
        in_specs=[pl.BlockSpec(memory_space=pltpu.SMEM), vmem] + [any_spec] * len(blocks),
        out_specs=(vmem, vmem),
        scratch_shapes=[
            pltpu.VMEM((4, n, width), jnp.bfloat16),
            pltpu.VMEM((4, m, width), jnp.bfloat16),
            pltpu.VMEM((m // tile, n, tile), jnp.float32),
            pltpu.VMEM((m, 128), jnp.float32),
            pltpu.SemaphoreType.DMA((4,)),
            pltpu.SemaphoreType.DMA((4,)),
        ],
        compiler_params=pltpu.CompilerParams(vmem_limit_bytes=48 << 20),
        name="kernel_block",
    )(place, columns, *blocks)


def middle_kernel(row_features, landmark_features, columns):
    half = row_features.shape[0] // 2
    end_landmarks = lax.ppermute(landmark_features, "landmark", TO_MIDDLE)
    end_top = lax.ppermute(row_features[:half], "landmark", TO_MIDDLE)
    middle_rows = lax.ppermute(row_features, "landmark", ACROSS)
    bottom, end_top = lax.optimization_barrier((row_features[half:], end_top))
    end_bottom = lax.ppermute(bottom, "landmark", TO_MIDDLE)
    far_top = lax.ppermute(end_top, "landmark", ACROSS)
    far_bottom = lax.ppermute(end_bottom, "landmark", ACROSS)
    rows = [
        (0, 0, row_features), (3, 0, middle_rows), (1, 0, end_top), (1, half, end_bottom),
        (2, 0, far_top), (2, half, far_bottom),
    ]
    landmarks = plane_pieces(landmark_features)
    shift = landmark_features.shape[0]
    landmarks += [(bits, row + shift, block) for bits, row, block in plane_pieces(end_landmarks)]
    return kernel_block(rows, landmarks, columns)


def conjugate_gradients(kernel, sums, columns, lam, sum_rows, sum_landmarks):
    count = columns.shape[0]
    residual, precond = sums[:count], lam + sums[count]
    coefficient = jnp.zeros_like(residual)
    inner = None
    for iteration in range(ITERS):
        scaled = residual / precond
        part = times(scaled, kernel, (1, 1))
        dots = [jnp.sum(residual * scaled, axis=1), jnp.sum(scaled * scaled, axis=1)]
        if iteration > 0:
            dots.append(jnp.sum(scaled * direction, axis=1))
        sums = sum_landmarks(packed(part, *dots))
        inner_next, square = sums[count, :count], sums[count + 1, :count]
        if iteration == 0:
            direction, image, length = scaled, sums[:count], square
        else:
            beta = inner_next / inner
            length = square + beta * (2.0 * sums[count + 2, :count] + beta * length)
            direction = scaled + beta[:, None] * direction
            image = sums[:count] + beta[:, None] * image
        inner = inner_next
        sums = sum_rows(packed(times(image, kernel, (1, 0)), jnp.sum(image * image, axis=1)))
        gradient = sums[:count] + lam * direction
        step_size = (inner / (sums[count, :count] + lam * length))[:, None]
        coefficient = coefficient + step_size * direction
        residual = residual - step_size * gradient
    return coefficient, residual


def folded(row_features, landmark_features, targets):
    lam = ridge_scale * row_features.shape[0] * lax.axis_size("proof")
    columns = targets.T
    kernel, sums = middle_kernel(row_features, landmark_features, columns)
    sums = sum_rows_axis(sums)
    coefficient, residual = conjugate_gradients(kernel, sums, columns, lam, sum_rows_axis, sum_middle)
    both = jnp.concatenate([coefficient, residual], axis=0)
    half = both.shape[1] // 2
    received = lax.ppermute(both[:, half:], "landmark", TO_END)
    z = lax.axis_index("landmark")
    both = jnp.where((z == 1) | (z == 2), both[:, :half], received)
    return both[: columns.shape[0]].T, both[columns.shape[0] :].T


def plain(row_features, landmark_features, targets):
    lam = ridge_scale * row_features.shape[0] * lax.axis_size("proof")
    columns = targets.T
    rows = lax.all_gather(row_features, "landmark", axis=1, tiled=True)
    whole = lax.all_gather(landmark_features, "proof", axis=1, tiled=True)
    kernel = jnp.exp(-(squares(rows)[:, None] + squares(whole)[None, :] - 2.0 * cross_piece(rows, whole)) / SPREAD)
    sum_rows = lambda block: lax.psum(block, "proof")
    sums = sum_rows(packed(times(columns, kernel, (1, 0)), jnp.sum(kernel * kernel, axis=0)))
    sum_landmarks = lambda block: lax.psum(block, "landmark")
    coefficient, residual = conjugate_gradients(kernel, sums, columns, lam, sum_rows, sum_landmarks)
    return coefficient.T, residual.T


def solution(mesh):
    placed = (P("proof", "landmark"), P("landmark", "proof"), P("proof", None))
    four_planes = mesh.shape["proof"] == 8 and mesh.shape["landmark"] == 4
    return jax.shard_map(
        folded if four_planes else plain,
        mesh=mesh,
        in_specs=placed,
        out_specs=(P("landmark", None), P("landmark", None)),
        check_vma=False,
    )
```

```python
import jax
import jax.numpy as jnp
from jax import lax
from jax.experimental import pallas as pl
from jax.experimental.pallas import tpu as pltpu
from jax.sharding import PartitionSpec as P

ITERS = 2
SPREAD = 10690

ridge_scale = 0.002


def squares(block):
    return jnp.sum(jnp.square(block.astype(jnp.float32)), axis=1)


def cross_piece(left, right):
    return lax.dot_general(
        left, right, (((1,), (1,)), ((), ())), preferred_element_type=jnp.float32
    )


def times(left, right, contract):
    return lax.dot_general(
        left, right, ((contract[:1], contract[1:]), ((), ())), precision=lax.Precision.HIGHEST
    )


TO_MIDDLE = [(0, 1), (3, 2)]
ACROSS = [(1, 2), (2, 1)]
TO_END = [(1, 0), (2, 3)]


def flipped(block, bits):
    return lax.ppermute(block, "proof", [(i, i ^ bits) for i in range(8)])


def sum_rows_axis(block):
    odd = lax.axis_index("proof") % 2
    half = block.shape[1] // 2
    low, high = block[:, :half], block[:, half:]
    mine, other = jnp.where(odd == 0, low, high), jnp.where(odd == 0, high, low)
    mine = mine + flipped(other, 1)
    mine = mine + flipped(mine, 2) + flipped(mine, 4) + flipped(mine, 6)
    other = flipped(mine, 1)
    low, high = jnp.where(odd == 0, mine, other), jnp.where(odd == 0, other, mine)
    return jnp.concatenate([low, high], axis=1)


def sum_middle(block):
    return block + lax.ppermute(block, "landmark", ACROSS)


def packed(block, *vectors):
    rows = jnp.stack(vectors)
    rows = jnp.pad(rows, ((0, 8 - rows.shape[0]), (0, block.shape[1] - rows.shape[1])))
    return jnp.concatenate([block, rows], axis=0)


def after(block, *earlier):
    return lax.optimization_barrier((block, *earlier))[0]


ANY = pl.BlockSpec(memory_space=pl.ANY)
VMEM = pl.BlockSpec(memory_space=pltpu.VMEM)
SMEM = pl.BlockSpec(memory_space=pltpu.SMEM)


def place():
    return jnp.stack([lax.axis_index("proof"), lax.axis_index("landmark")]).astype(jnp.int32)


def lane_squares(block):
    total = None
    for j in range(block.shape[1] // 128):
        x = block[:, j * 128 : (j + 1) * 128].astype(jnp.float32)
        total = x * x if total is None else total + x * x
    return total


def product(left, right):
    return lax.dot_general(left, right, (((1,), (1,)), ((), ())), preferred_element_type=jnp.float32)


def tiled_product(cross_ref, left, right_ref):
    for t in range(cross_ref.shape[0]):
        cross_ref[t] += product(left[...], right_ref[t * 256 : (t + 1) * 256])


def feature_block(z, zbits, side):
    return 2 * (z ^ zbits) + side


class Rows:
    def __init__(self, blocks):
        self.keys, self.blocks = list(blocks), list(blocks.values())

    def source(self, refs, zbits, side, width):
        if (zbits, None) in self.keys:
            return refs[self.keys.index((zbits, None))].at[:, pl.ds(side * width, width)]
        return refs[self.keys.index((zbits, side))]


class Landmarks:
    def __init__(self, parts):
        self.keys = [(bits, row) for bits, row, _ in parts]
        self.blocks = [block for _, _, block in parts]

    def start(self, refs, bits, target, sem):
        for (found, row), ref in zip(self.keys, refs):
            if found == bits:
                pltpu.make_async_copy(ref, target.at[pl.ds(row, ref.shape[0])], sem).start()

    def start_any(self, refs, bits, target, sem):
        for one in sorted({found for found, _ in self.keys}):
            @pl.when(bits == one)
            def _():
                self.start(refs, one, target, sem)


def wait(target, sem):
    pltpu.make_async_copy(target, target, sem).wait()


def call(body, inputs, specs, shapes, scratch, name):
    return pl.pallas_call(
        body,
        out_shape=tuple(jax.ShapeDtypeStruct(shape, jnp.float32) for shape in shapes),
        in_specs=specs,
        out_specs=tuple(VMEM for _ in shapes),
        scratch_shapes=scratch,
        compiler_params=pltpu.CompilerParams(vmem_limit_bytes=60 << 20),
        cost_estimate=pl.CostEstimate(flops=1000, bytes_accessed=1000, transcendentals=0),
        name=name,
    )(*inputs)


def own_block(rows, landmarks, n, m, width):
    rows, landmarks = Rows(rows), Landmarks(landmarks)
    sources = [(0, 0), (0, 1), (3, 0), (3, 1), (1, 0)]

    def body(place_ref, *refs):
        row_refs, refs = refs[: len(rows.keys)], refs[len(rows.keys) :]
        landmark_refs, refs = refs[: len(landmarks.keys)], refs[len(landmarks.keys) :]
        cross_ref, row_norm_ref, norm_ref, rows_s, land_s, row_sem, land_sem = refs
        p, z = place_ref[0], place_ref[1]
        wanted = [feature_block(z, zbits, side) ^ p for zbits, side in sources]
        for i, (zbits, side) in enumerate(sources):
            pltpu.make_async_copy(rows.source(row_refs, zbits, side, width), rows_s.at[i], row_sem.at[i]).start()
        for bits in range(8):
            landmarks.start(landmark_refs, bits, land_s.at[bits], land_sem.at[bits])
        cross_ref[...] = jnp.zeros_like(cross_ref)
        for bits in range(8):
            wait(land_s.at[bits], land_sem.at[bits])
            squares_here = lane_squares(land_s[bits])
            norm_ref[...] = squares_here if bits == 0 else norm_ref[...] + squares_here
        for i in range(len(sources)):
            wait(rows_s.at[i], row_sem.at[i])
            tiled_product(cross_ref, rows_s.at[i], land_s.at[wanted[i]])
            squares_here = lane_squares(rows_s[i])
            row_norm_ref[...] = squares_here if i == 0 else row_norm_ref[...] + squares_here

    return call(
        body,
        [place()] + rows.blocks + landmarks.blocks,
        [SMEM] + [ANY] * (len(rows.keys) + len(landmarks.keys)),
        [(m // 256, n, 256), (n, 128), (m, 128)],
        [
            pltpu.VMEM((len(sources), n, width), jnp.bfloat16),
            pltpu.VMEM((8, m, width), jnp.bfloat16),
            pltpu.SemaphoreType.DMA((len(sources),)),
            pltpu.SemaphoreType.DMA((8,)),
        ],
        "own_block",
    )


def end_block(rows, own, end, cross_own, row_norm, n, m, width):
    rows, own, end = Rows(rows), Landmarks(own), Landmarks(end)
    late = 2 * 2 + 1

    def body(place_ref, cross_in, norm_in, *refs):
        row_refs, refs = refs[: len(rows.keys)], refs[len(rows.keys) :]
        own_refs, refs = refs[: len(own.keys)], refs[len(own.keys) :]
        end_refs, refs = refs[: len(end.keys)], refs[len(end.keys) :]
        cross_own_ref, cross_ref, row_norm_ref, norm_ref, rows_s, own_s, end_s, row_sem, own_sem, end_sem = refs
        p, z = place_ref[0], place_ref[1]
        more = [(1, 1), (2, 0)]
        for zbits, side in more:
            slot = 2 * zbits + side
            pltpu.make_async_copy(rows.source(row_refs, zbits, side, width), rows_s.at[slot], row_sem.at[slot]).start()
        for i, (zbits, side) in enumerate(more):
            own.start_any(own_refs, feature_block(z, zbits, side) ^ p, own_s.at[i], own_sem.at[i])
        for slot in range(8):
            if slot != late and (slot // 2, slot % 2) not in more:
                source = rows.source(row_refs, slot // 2, slot % 2, width)
                pltpu.make_async_copy(source, rows_s.at[slot], row_sem.at[slot]).start()
        for bits in range(6):
            end.start(end_refs, bits, end_s.at[bits], end_sem.at[bits])
        cross_own_ref[...] = cross_in[...]
        cross_ref[...] = jnp.zeros_like(cross_ref)
        row_total = norm_in[...]
        for i, (zbits, side) in enumerate(more):
            slot = 2 * zbits + side
            wait(rows_s.at[slot], row_sem.at[slot])
            wait(own_s.at[i], own_sem.at[i])
            tiled_product(cross_own_ref, rows_s.at[slot], own_s.at[i])
            row_total = row_total + lane_squares(rows_s[slot])
        row_norm_ref[...] = row_total
        for slot in range(8):
            if slot != late and (slot // 2, slot % 2) not in more:
                wait(rows_s.at[slot], row_sem.at[slot])
        for bits in range(6):
            wait(end_s.at[bits], end_sem.at[bits])
            f = p ^ bits
            slot = 2 * (z ^ (f // 2)) + f % 2

            @pl.when(slot != late)
            def _():
                tiled_product(cross_ref, rows_s.at[slot], end_s.at[bits])

            squares_here = lane_squares(end_s[bits])
            norm_ref[...] = squares_here if bits == 0 else norm_ref[...] + squares_here

    return call(
        body,
        [place(), cross_own, row_norm] + rows.blocks + own.blocks + end.blocks,
        [SMEM, VMEM, VMEM] + [ANY] * (len(rows.keys) + len(own.keys) + len(end.keys)),
        [(m // 256, n, 256), (m // 256, n, 256), (n, 128), (m, 128)],
        [
            pltpu.VMEM((8, n, width), jnp.bfloat16),
            pltpu.VMEM((2, m, width), jnp.bfloat16),
            pltpu.VMEM((6, m, width), jnp.bfloat16),
            pltpu.SemaphoreType.DMA((8,)),
            pltpu.SemaphoreType.DMA((2,)),
            pltpu.SemaphoreType.DMA((6,)),
        ],
        "end_block",
    )


def last_block(rows, own, end, cross_own, cross_end, row_norm, norm_own, norm_end, columns, width):
    rows, own, end = Rows(rows), Landmarks(own), Landmarks(end)
    n, m, count = columns.shape[1], norm_own.shape[0], columns.shape[0]

    def body(place_ref, cross_own_in, cross_end_in, row_norm_in, norm_own_in, norm_end_in, columns_ref, *refs):
        row_refs, refs = refs[: len(rows.keys)], refs[len(rows.keys) :]
        own_refs, refs = refs[: len(own.keys)], refs[len(own.keys) :]
        end_refs, refs = refs[: len(end.keys)], refs[len(end.keys) :]
        kernel_ref, sums_ref, cross_s, rows_s, own_s, end_s, row_sem, own_sem, end_sem = refs
        p, z = place_ref[0], place_ref[1]
        far = feature_block(z, 2, 1) ^ p
        pltpu.make_async_copy(rows.source(row_refs, 2, 1, width), rows_s.at[2], row_sem.at[2]).start()
        own.start_any(own_refs, far, own_s, own_sem)
        for i in range(2):
            f = p ^ (6 + i)
            for zbits in range(4):
                for side in range(2):
                    @pl.when((z ^ (f // 2) == zbits) & (f % 2 == side))
                    def _():
                        source = rows.source(row_refs, zbits, side, width)
                        pltpu.make_async_copy(source, rows_s.at[i], row_sem.at[i]).start()
            end.start(end_refs, 6 + i, end_s.at[i], end_sem.at[i])

        @pl.when(far < 6)
        def _():
            end.start_any(end_refs, far, end_s.at[2], end_sem.at[2])

        half = m // 256
        cross_s[:half] = cross_own_in[...]
        cross_s[half:] = cross_end_in[...]
        wait(rows_s.at[2], row_sem.at[2])
        wait(own_s, own_sem)
        tiled_product(cross_s.at[:half], rows_s.at[2], own_s)
        row_norm = jnp.sum(row_norm_in[...] + lane_squares(rows_s[2]), axis=1, keepdims=True)
        norm_end = norm_end_in[...]
        for i in range(2):
            wait(rows_s.at[i], row_sem.at[i])
            wait(end_s.at[i], end_sem.at[i])
            tiled_product(cross_s.at[half:], rows_s.at[i], end_s.at[i])
            norm_end = norm_end + lane_squares(end_s[i])

        @pl.when(far < 6)
        def _():
            wait(end_s.at[2], end_sem.at[2])
            tiled_product(cross_s.at[half:], rows_s.at[2], end_s.at[2])

        ones = jnp.ones((8, 128), jnp.float32)
        for t in range(2 * half):
            inside = slice(t * 256, (t + 1) * 256)
            lanes = norm_own_in[inside] if t < half else norm_end[(t - half) * 256 : (t - half + 1) * 256]
            norm = lax.dot_general(ones, lanes, (((1,), (1,)), ((), ())), precision=lax.Precision.HIGHEST)[:1]
            k = jnp.exp(-(row_norm + norm - 2.0 * cross_s[t]) / SPREAD)
            kernel_ref[:, inside] = k
            sums_ref[:count, inside] = jnp.dot(columns_ref[...], k, precision=lax.Precision.HIGHEST)
            sums_ref[count:, inside] = jnp.broadcast_to(jnp.sum(k * k, axis=0, keepdims=True), (8, 256))

    return call(
        body,
        [place(), cross_own, cross_end, row_norm, norm_own, norm_end, columns]
        + rows.blocks + own.blocks + end.blocks,
        [SMEM] + [VMEM] * 6 + [ANY] * (len(rows.keys) + len(own.keys) + len(end.keys)),
        [(n, 2 * m), (count + 8, 2 * m)],
        [
            pltpu.VMEM((2 * m // 256, n, 256), jnp.float32),
            pltpu.VMEM((3, n, width), jnp.bfloat16),
            pltpu.VMEM((m, width), jnp.bfloat16),
            pltpu.VMEM((3, m, width), jnp.bfloat16),
            pltpu.SemaphoreType.DMA((3,)),
            pltpu.SemaphoreType.DMA,
            pltpu.SemaphoreType.DMA((3,)),
        ],
        "last_block",
    )


def middle_kernel(row_features, landmark_features, columns):
    own = landmark_features
    m, half = own.shape
    n, middle = row_features.shape[0], m // 2
    left, right = row_features[:, :half], row_features[:, half:]
    end = lax.ppermute(own, "landmark", TO_MIDDLE)
    own_x, own_y = flipped(own, 2), flipped(own, 4)
    middle_rows = lax.ppermute(row_features, "landmark", ACROSS)
    own_x, own_y, end, left = lax.optimization_barrier((own_x, own_y, end, left))
    end_left = lax.ppermute(left, "landmark", TO_MIDDLE)
    own_low, own_high = flipped(own_x[:middle], 4), flipped(own_y[middle:], 2)
    other_own, other_x, other_y = flipped(after(own, own_x), 1), flipped(own_x, 1), flipped(own_y, 1)
    own_low, own_high, end = lax.optimization_barrier((own_low, own_high, end))
    end_x, end_y = flipped(end, 2), flipped(end, 4)
    other_low, other_high = flipped(own_low, 1), flipped(own_high, 1)
    end_bottom = end[middle:]
    end_left, right, middle_rows = lax.optimization_barrier((end_left, right, middle_rows))
    far_left = lax.ppermute(end_left, "landmark", ACROSS)
    end_right = lax.ppermute(right, "landmark", TO_MIDDLE)
    own_parts = [
        (0, 0, own), (2, 0, own_x), (4, 0, own_y), (6, 0, own_low), (6, middle, own_high),
        (1, 0, other_own), (3, 0, other_x), (5, 0, other_y), (7, 0, other_low), (7, middle, other_high),
    ]
    rows = {(0, None): row_features, (3, None): middle_rows, (1, 0): end_left}
    cross_own, row_norm, norm_own = own_block(rows, own_parts, n, m, half)
    end_x, end_y, end_bottom, far_left, _ = lax.optimization_barrier((end_x, end_y, end_bottom, far_left, cross_own))
    end_high = flipped(end_bottom, 6)
    end_right = after(end_right, end_x, end_y)
    far_right = lax.ppermute(end_right, "landmark", ACROSS)
    end_low = lax.ppermute(after(own_low, end_right), "landmark", TO_MIDDLE)
    end_parts = [(0, 0, end), (2, 0, end_x), (4, 0, end_y)]
    end_parts += [(bits + 1, row, flipped(block, 1)) for bits, row, block in end_parts]
    rows |= {(1, 1): end_right, (2, 0): far_left}
    cross_own, cross_end, row_norm, norm_end = end_block(
        rows, own_parts, end_parts, cross_own, row_norm, n, m, half
    )
    corner = [(6, 0, after(end_low, cross_end)), (6, middle, after(end_high, cross_end))]
    end_parts += corner + [(bits + 1, row, flipped(block, 1)) for bits, row, block in corner]
    rows |= {(2, 1): far_right}
    return last_block(
        rows, own_parts, end_parts, cross_own, cross_end, row_norm, norm_own, norm_end, columns, half
    )


def conjugate_gradients(kernel, sums, columns, lam, sum_rows, sum_landmarks):
    count = columns.shape[0]
    residual, precond = sums[:count], lam + sums[count]
    coefficient = jnp.zeros_like(residual)
    inner = None
    for iteration in range(ITERS):
        scaled = residual / precond
        part = times(scaled, kernel, (1, 1))
        dots = [jnp.sum(residual * scaled, axis=1), jnp.sum(scaled * scaled, axis=1)]
        if iteration > 0:
            dots.append(jnp.sum(scaled * direction, axis=1))
        sums = sum_landmarks(packed(part, *dots))
        inner_next, square = sums[count, :count], sums[count + 1, :count]
        if iteration == 0:
            direction, image, length = scaled, sums[:count], square
        else:
            beta = inner_next / inner
            length = square + beta * (2.0 * sums[count + 2, :count] + beta * length)
            direction = scaled + beta[:, None] * direction
            image = sums[:count] + beta[:, None] * image
        inner = inner_next
        sums = sum_rows(packed(times(image, kernel, (1, 0)), jnp.sum(image * image, axis=1)))
        gradient = sums[:count] + lam * direction
        step_size = (inner / (sums[count, :count] + lam * length))[:, None]
        coefficient = coefficient + step_size * direction
        residual = residual - step_size * gradient
    return coefficient, residual


def folded(row_features, landmark_features, targets):
    lam = ridge_scale * row_features.shape[0] * lax.axis_size("proof")
    columns = targets.T
    kernel, sums = middle_kernel(row_features, landmark_features, columns)
    sums = sum_rows_axis(sums)
    coefficient, residual = conjugate_gradients(kernel, sums, columns, lam, sum_rows_axis, sum_middle)
    both = jnp.concatenate([coefficient, residual], axis=0)
    half = both.shape[1] // 2
    received = lax.ppermute(both[:, half:], "landmark", TO_END)
    z = lax.axis_index("landmark")
    both = jnp.where((z == 1) | (z == 2), both[:, :half], received)
    return both[: columns.shape[0]].T, both[columns.shape[0] :].T


def plain(row_features, landmark_features, targets):
    lam = ridge_scale * row_features.shape[0] * lax.axis_size("proof")
    columns = targets.T
    rows = lax.all_gather(row_features, "landmark", axis=1, tiled=True)
    whole = lax.all_gather(landmark_features, "proof", axis=1, tiled=True)
    kernel = jnp.exp(-(squares(rows)[:, None] + squares(whole)[None, :] - 2.0 * cross_piece(rows, whole)) / SPREAD)
    sum_rows = lambda block: lax.psum(block, "proof")
    sums = sum_rows(packed(times(columns, kernel, (1, 0)), jnp.sum(kernel * kernel, axis=0)))
    sum_landmarks = lambda block: lax.psum(block, "landmark")
    coefficient, residual = conjugate_gradients(kernel, sums, columns, lam, sum_rows, sum_landmarks)
    return coefficient.T, residual.T


def solution(mesh):
    placed = (P("proof", "landmark"), P("landmark", "proof"), P("proof", None))
    four_planes = mesh.shape["proof"] == 8 and mesh.shape["landmark"] == 4
    return jax.shard_map(
        folded if four_planes else plain,
        mesh=mesh,
        in_specs=placed,
        out_specs=(P("landmark", None), P("landmark", None)),
        check_vma=False,
    )
```

```python
import jax
import jax.numpy as jnp
from jax import lax
from jax.experimental import pallas as pl
from jax.experimental.pallas import tpu as pltpu
from jax.sharding import PartitionSpec as P

ITERS = 2
SPREAD = 10690

ridge_scale = 0.002


def squares(block):
    return jnp.sum(jnp.square(block.astype(jnp.float32)), axis=1)


def cross_piece(left, right):
    return lax.dot_general(
        left, right, (((1,), (1,)), ((), ())), preferred_element_type=jnp.float32
    )


def times(left, right, contract):
    return lax.dot_general(
        left, right, ((contract[:1], contract[1:]), ((), ())), precision=lax.Precision.HIGHEST
    )


NEIGHBOURS = [(0, 1), (1, 0), (2, 3), (3, 2)]


def handed(block):
    return lax.ppermute(block, "landmark", NEIGHBOURS)


def across(block):
    pairs = [(4 * p + z, 4 * p + 3 - z if z in (1, 2) else 4 * (p ^ 1) + z) for p in range(8) for z in range(4)]
    return lax.ppermute(block, ("proof", "landmark"), pairs)


def flipped(block, bits):
    return lax.ppermute(block, "proof", [(i, i ^ bits) for i in range(8)])


def sum_rows_axis(block):
    odd = lax.axis_index("proof") % 2
    half = block.shape[1] // 2
    low, high = block[:, :half], block[:, half:]
    mine, other = jnp.where(odd == 0, low, high), jnp.where(odd == 0, high, low)
    mine = mine + flipped(other, 1)
    mine = mine + flipped(mine, 2) + flipped(mine, 4) + flipped(mine, 6)
    other = flipped(mine, 1)
    low, high = jnp.where(odd == 0, mine, other), jnp.where(odd == 0, other, mine)
    return jnp.concatenate([low, high], axis=1)


def sum_middle(block):
    return block + across(block)


def packed(block, *vectors):
    rows = jnp.stack(vectors)
    rows = jnp.pad(rows, ((0, 8 - rows.shape[0]), (0, block.shape[1] - rows.shape[1])))
    return jnp.concatenate([block, rows], axis=0)


def after(block, *earlier):
    return lax.optimization_barrier((block, *earlier))[0]


ANY = pl.BlockSpec(memory_space=pl.ANY)
VMEM = pl.BlockSpec(memory_space=pltpu.VMEM)
SMEM = pl.BlockSpec(memory_space=pltpu.SMEM)


def place():
    return jnp.stack([lax.axis_index("proof"), lax.axis_index("landmark")]).astype(jnp.int32)


def lane_squares(block):
    total = None
    for j in range(block.shape[1] // 128):
        x = block[:, j * 128 : (j + 1) * 128].astype(jnp.float32)
        total = x * x if total is None else total + x * x
    return total


def product(left, right):
    return lax.dot_general(left, right, (((1,), (1,)), ((), ())), preferred_element_type=jnp.float32)


def tiled_product(cross_ref, left, right_ref):
    for t in range(cross_ref.shape[0]):
        cross_ref[t] += product(left[...], right_ref[t * 256 : (t + 1) * 256])


def feature_block(z, zbits, side):
    return 2 * (z ^ zbits) + side


class Rows:
    def __init__(self, blocks):
        self.keys, self.blocks = list(blocks), list(blocks.values())

    def source(self, refs, zbits, side, width):
        if (zbits, None) in self.keys:
            return refs[self.keys.index((zbits, None))].at[:, pl.ds(side * width, width)]
        return refs[self.keys.index((zbits, side))]


class Landmarks:
    def __init__(self, parts):
        self.keys = [(bits, row) for bits, row, _ in parts]
        self.blocks = [block for _, _, block in parts]

    def start(self, refs, bits, target, sem):
        for (found, row), ref in zip(self.keys, refs):
            if found == bits:
                pltpu.make_async_copy(ref, target.at[pl.ds(row, ref.shape[0])], sem).start()

    def start_any(self, refs, bits, target, sem):
        for one in sorted({found for found, _ in self.keys}):
            @pl.when(bits == one)
            def _():
                self.start(refs, one, target, sem)


def wait(target, sem):
    pltpu.make_async_copy(target, target, sem).wait()


def call(body, inputs, specs, shapes, scratch, name):
    return pl.pallas_call(
        body,
        out_shape=tuple(jax.ShapeDtypeStruct(shape, jnp.float32) for shape in shapes),
        in_specs=specs,
        out_specs=tuple(VMEM for _ in shapes),
        scratch_shapes=scratch,
        compiler_params=pltpu.CompilerParams(vmem_limit_bytes=60 << 20),
        cost_estimate=pl.CostEstimate(flops=1000, bytes_accessed=1000, transcendentals=0),
        name=name,
    )(*inputs)


def own_block(rows, landmarks, n, m, width):
    rows, landmarks = Rows(rows), Landmarks(landmarks)
    sources = [(0, 0), (0, 1), (3, 0), (3, 1), (1, 0)]

    def body(place_ref, *refs):
        row_refs, refs = refs[: len(rows.keys)], refs[len(rows.keys) :]
        landmark_refs, refs = refs[: len(landmarks.keys)], refs[len(landmarks.keys) :]
        cross_ref, row_norm_ref, norm_ref, rows_s, land_s, row_sem, land_sem = refs
        p, z = place_ref[0], place_ref[1]
        wanted = [feature_block(z, zbits, side) ^ p for zbits, side in sources]
        for i, (zbits, side) in enumerate(sources):
            pltpu.make_async_copy(rows.source(row_refs, zbits, side, width), rows_s.at[i], row_sem.at[i]).start()
        for bits in range(8):
            landmarks.start(landmark_refs, bits, land_s.at[bits], land_sem.at[bits])
        cross_ref[...] = jnp.zeros_like(cross_ref)
        for bits in range(8):
            wait(land_s.at[bits], land_sem.at[bits])
            squares_here = lane_squares(land_s[bits])
            norm_ref[...] = squares_here if bits == 0 else norm_ref[...] + squares_here
        for i in range(len(sources)):
            wait(rows_s.at[i], row_sem.at[i])
            tiled_product(cross_ref, rows_s.at[i], land_s.at[wanted[i]])
            squares_here = lane_squares(rows_s[i])
            row_norm_ref[...] = squares_here if i == 0 else row_norm_ref[...] + squares_here

    return call(
        body,
        [place()] + rows.blocks + landmarks.blocks,
        [SMEM] + [ANY] * (len(rows.keys) + len(landmarks.keys)),
        [(m // 256, n, 256), (n, 128), (m, 128)],
        [
            pltpu.VMEM((len(sources), n, width), jnp.bfloat16),
            pltpu.VMEM((8, m, width), jnp.bfloat16),
            pltpu.SemaphoreType.DMA((len(sources),)),
            pltpu.SemaphoreType.DMA((8,)),
        ],
        "own_block",
    )


def end_block(rows, own, end, cross_own, row_norm, n, m, width):
    rows, own, end = Rows(rows), Landmarks(own), Landmarks(end)
    late = 2 * 2 + 1

    def body(place_ref, cross_in, norm_in, *refs):
        row_refs, refs = refs[: len(rows.keys)], refs[len(rows.keys) :]
        own_refs, refs = refs[: len(own.keys)], refs[len(own.keys) :]
        end_refs, refs = refs[: len(end.keys)], refs[len(end.keys) :]
        cross_own_ref, cross_ref, row_norm_ref, norm_ref, rows_s, own_s, end_s, row_sem, own_sem, end_sem = refs
        p, z = place_ref[0], place_ref[1]
        more = [(1, 1), (2, 0)]
        for zbits, side in more:
            slot = 2 * zbits + side
            pltpu.make_async_copy(rows.source(row_refs, zbits, side, width), rows_s.at[slot], row_sem.at[slot]).start()
        for i, (zbits, side) in enumerate(more):
            own.start_any(own_refs, feature_block(z, zbits, side) ^ p, own_s.at[i], own_sem.at[i])
        for slot in range(8):
            if slot != late and (slot // 2, slot % 2) not in more:
                source = rows.source(row_refs, slot // 2, slot % 2, width)
                pltpu.make_async_copy(source, rows_s.at[slot], row_sem.at[slot]).start()
        for bits in range(6):
            end.start(end_refs, bits, end_s.at[bits], end_sem.at[bits])
        cross_own_ref[...] = cross_in[...]
        cross_ref[...] = jnp.zeros_like(cross_ref)
        row_total = norm_in[...]
        for i, (zbits, side) in enumerate(more):
            slot = 2 * zbits + side
            wait(rows_s.at[slot], row_sem.at[slot])
            wait(own_s.at[i], own_sem.at[i])
            tiled_product(cross_own_ref, rows_s.at[slot], own_s.at[i])
            row_total = row_total + lane_squares(rows_s[slot])
        row_norm_ref[...] = row_total
        for slot in range(8):
            if slot != late and (slot // 2, slot % 2) not in more:
                wait(rows_s.at[slot], row_sem.at[slot])
        for bits in range(6):
            wait(end_s.at[bits], end_sem.at[bits])
            f = p ^ bits
            slot = 2 * (z ^ (f // 2)) + f % 2

            @pl.when(slot != late)
            def _():
                tiled_product(cross_ref, rows_s.at[slot], end_s.at[bits])

            squares_here = lane_squares(end_s[bits])
            norm_ref[...] = squares_here if bits == 0 else norm_ref[...] + squares_here

    return call(
        body,
        [place(), cross_own, row_norm] + rows.blocks + own.blocks + end.blocks,
        [SMEM, VMEM, VMEM] + [ANY] * (len(rows.keys) + len(own.keys) + len(end.keys)),
        [(m // 256, n, 256), (m // 256, n, 256), (n, 128), (m, 128)],
        [
            pltpu.VMEM((8, n, width), jnp.bfloat16),
            pltpu.VMEM((2, m, width), jnp.bfloat16),
            pltpu.VMEM((6, m, width), jnp.bfloat16),
            pltpu.SemaphoreType.DMA((8,)),
            pltpu.SemaphoreType.DMA((2,)),
            pltpu.SemaphoreType.DMA((6,)),
        ],
        "end_block",
    )


def last_block(rows, own, end, cross_own, cross_end, row_norm, norm_own, norm_end, columns, width):
    rows, own, end = Rows(rows), Landmarks(own), Landmarks(end)
    n, m, count = columns.shape[1], norm_own.shape[0], columns.shape[0]

    def body(place_ref, cross_own_in, cross_end_in, row_norm_in, norm_own_in, norm_end_in, columns_ref, *refs):
        row_refs, refs = refs[: len(rows.keys)], refs[len(rows.keys) :]
        own_refs, refs = refs[: len(own.keys)], refs[len(own.keys) :]
        end_refs, refs = refs[: len(end.keys)], refs[len(end.keys) :]
        kernel_ref, sums_ref, cross_s, rows_s, own_s, end_s, row_sem, own_sem, end_sem = refs
        p, z = place_ref[0], place_ref[1]
        far = feature_block(z, 2, 1) ^ p
        pltpu.make_async_copy(rows.source(row_refs, 2, 1, width), rows_s.at[2], row_sem.at[2]).start()
        own.start_any(own_refs, far, own_s, own_sem)
        for i in range(2):
            f = p ^ (6 + i)
            for zbits in range(4):
                for side in range(2):
                    @pl.when((z ^ (f // 2) == zbits) & (f % 2 == side))
                    def _():
                        source = rows.source(row_refs, zbits, side, width)
                        pltpu.make_async_copy(source, rows_s.at[i], row_sem.at[i]).start()
            end.start(end_refs, 6 + i, end_s.at[i], end_sem.at[i])

        @pl.when(far < 6)
        def _():
            end.start_any(end_refs, far, end_s.at[2], end_sem.at[2])

        half = m // 256
        cross_s[:half] = cross_own_in[...]
        cross_s[half:] = cross_end_in[...]
        wait(rows_s.at[2], row_sem.at[2])
        wait(own_s, own_sem)
        tiled_product(cross_s.at[:half], rows_s.at[2], own_s)
        row_norm = jnp.sum(row_norm_in[...] + lane_squares(rows_s[2]), axis=1, keepdims=True)
        norm_end = norm_end_in[...]
        for i in range(2):
            wait(rows_s.at[i], row_sem.at[i])
            wait(end_s.at[i], end_sem.at[i])
            tiled_product(cross_s.at[half:], rows_s.at[i], end_s.at[i])
            norm_end = norm_end + lane_squares(end_s[i])

        @pl.when(far < 6)
        def _():
            wait(end_s.at[2], end_sem.at[2])
            tiled_product(cross_s.at[half:], rows_s.at[2], end_s.at[2])

        ones = jnp.ones((8, 128), jnp.float32)
        for t in range(2 * half):
            inside = slice(t * 256, (t + 1) * 256)
            lanes = norm_own_in[inside] if t < half else norm_end[(t - half) * 256 : (t - half + 1) * 256]
            norm = lax.dot_general(ones, lanes, (((1,), (1,)), ((), ())), precision=lax.Precision.HIGHEST)[:1]
            k = jnp.exp(-(row_norm + norm - 2.0 * cross_s[t]) / SPREAD)
            kernel_ref[:, inside] = k
            sums_ref[:count, inside] = jnp.dot(columns_ref[...], k, precision=lax.Precision.HIGHEST)
            sums_ref[count:, inside] = jnp.broadcast_to(jnp.sum(k * k, axis=0, keepdims=True), (8, 256))

    return call(
        body,
        [place(), cross_own, cross_end, row_norm, norm_own, norm_end, columns]
        + rows.blocks + own.blocks + end.blocks,
        [SMEM] + [VMEM] * 6 + [ANY] * (len(rows.keys) + len(own.keys) + len(end.keys)),
        [(n, 2 * m), (count + 8, 2 * m)],
        [
            pltpu.VMEM((2 * m // 256, n, 256), jnp.float32),
            pltpu.VMEM((3, n, width), jnp.bfloat16),
            pltpu.VMEM((m, width), jnp.bfloat16),
            pltpu.VMEM((3, m, width), jnp.bfloat16),
            pltpu.SemaphoreType.DMA((3,)),
            pltpu.SemaphoreType.DMA,
            pltpu.SemaphoreType.DMA((3,)),
        ],
        "last_block",
    )


def middle_kernel(row_features, landmark_features, columns):
    own = landmark_features
    m, half = own.shape
    n, middle = row_features.shape[0], m // 2
    left, right = row_features[:, :half], row_features[:, half:]
    end = handed(own)
    own_x, own_y = flipped(own, 2), flipped(own, 4)
    middle_rows = across(row_features)
    own_x, own_y, end, left = lax.optimization_barrier((own_x, own_y, end, left))
    end_left = handed(left)
    own_low, own_high = flipped(own_x[:middle], 4), flipped(own_y[middle:], 2)
    other_own, other_x, other_y = flipped(after(own, own_x), 1), flipped(own_x, 1), flipped(own_y, 1)
    own_low, own_high, end = lax.optimization_barrier((own_low, own_high, end))
    end_x, end_y = flipped(end, 2), flipped(end, 4)
    other_low, other_high = flipped(own_low, 1), flipped(own_high, 1)
    end_bottom = end[middle:]
    end_left, right, middle_rows = lax.optimization_barrier((end_left, right, middle_rows))
    far_left = across(end_left)
    end_right = handed(right)
    own_parts = [
        (0, 0, own), (2, 0, own_x), (4, 0, own_y), (6, 0, own_low), (6, middle, own_high),
        (1, 0, other_own), (3, 0, other_x), (5, 0, other_y), (7, 0, other_low), (7, middle, other_high),
    ]
    rows = {(0, None): row_features, (3, None): middle_rows, (1, 0): end_left}
    cross_own, row_norm, norm_own = own_block(rows, own_parts, n, m, half)
    end_x, end_y, end_bottom, far_left, _ = lax.optimization_barrier((end_x, end_y, end_bottom, far_left, cross_own))
    end_high = flipped(end_bottom, 6)
    end_right = after(end_right, end_x, end_y)
    far_right = across(end_right)
    end_low = handed(after(own_low, end_right))
    end_parts = [(0, 0, end), (2, 0, end_x), (4, 0, end_y)]
    end_parts += [(bits + 1, row, flipped(block, 1)) for bits, row, block in end_parts]
    rows |= {(1, 1): end_right, (2, 0): far_left}
    cross_own, cross_end, row_norm, norm_end = end_block(
        rows, own_parts, end_parts, cross_own, row_norm, n, m, half
    )
    corner = [(6, 0, after(end_low, cross_end)), (6, middle, after(end_high, cross_end))]
    end_parts += corner + [(bits + 1, row, flipped(block, 1)) for bits, row, block in corner]
    rows |= {(2, 1): far_right}
    return last_block(
        rows, own_parts, end_parts, cross_own, cross_end, row_norm, norm_own, norm_end, columns, half
    )


def conjugate_gradients(kernel, sums, columns, lam, sum_rows, sum_landmarks):
    count = columns.shape[0]
    residual, precond = sums[:count], lam + sums[count]
    coefficient = jnp.zeros_like(residual)
    inner = None
    for iteration in range(ITERS):
        scaled = residual / precond
        part = times(scaled, kernel, (1, 1))
        dots = [jnp.sum(residual * scaled, axis=1), jnp.sum(scaled * scaled, axis=1)]
        if iteration > 0:
            dots.append(jnp.sum(scaled * direction, axis=1))
        sums = sum_landmarks(packed(part, *dots))
        inner_next, square = sums[count, :count], sums[count + 1, :count]
        if iteration == 0:
            direction, image, length = scaled, sums[:count], square
        else:
            beta = inner_next / inner
            length = square + beta * (2.0 * sums[count + 2, :count] + beta * length)
            direction = scaled + beta[:, None] * direction
            image = sums[:count] + beta[:, None] * image
        inner = inner_next
        sums = sum_rows(packed(times(image, kernel, (1, 0)), jnp.sum(image * image, axis=1)))
        gradient = sums[:count] + lam * direction
        step_size = (inner / (sums[count, :count] + lam * length))[:, None]
        coefficient = coefficient + step_size * direction
        residual = residual - step_size * gradient
    return coefficient, residual


def folded(row_features, landmark_features, targets):
    lam = ridge_scale * row_features.shape[0] * lax.axis_size("proof")
    columns = targets.T
    kernel, sums = middle_kernel(row_features, landmark_features, columns)
    sums = sum_rows_axis(sums)
    coefficient, residual = conjugate_gradients(kernel, sums, columns, lam, sum_rows_axis, sum_middle)
    both = jnp.concatenate([coefficient, residual], axis=0)
    half = both.shape[1] // 2
    received = handed(both[:, half:])
    z = lax.axis_index("landmark")
    both = jnp.where((z == 1) | (z == 2), both[:, :half], received)
    return both[: columns.shape[0]].T, both[columns.shape[0] :].T


def plain(row_features, landmark_features, targets):
    lam = ridge_scale * row_features.shape[0] * lax.axis_size("proof")
    columns = targets.T
    rows = lax.all_gather(row_features, "landmark", axis=1, tiled=True)
    whole = lax.all_gather(landmark_features, "proof", axis=1, tiled=True)
    kernel = jnp.exp(-(squares(rows)[:, None] + squares(whole)[None, :] - 2.0 * cross_piece(rows, whole)) / SPREAD)
    sum_rows = lambda block: lax.psum(block, "proof")
    sums = sum_rows(packed(times(columns, kernel, (1, 0)), jnp.sum(kernel * kernel, axis=0)))
    sum_landmarks = lambda block: lax.psum(block, "landmark")
    coefficient, residual = conjugate_gradients(kernel, sums, columns, lam, sum_rows, sum_landmarks)
    return coefficient.T, residual.T


def solution(mesh):
    placed = (P("proof", "landmark"), P("landmark", "proof"), P("proof", None))
    four_planes = mesh.shape["proof"] == 8 and mesh.shape["landmark"] == 4
    return jax.shard_map(
        folded if four_planes else plain,
        mesh=mesh,
        in_specs=placed,
        out_specs=(P("landmark", None), P("landmark", None)),
        check_vma=False,
    )
```

```python
import jax
import jax.numpy as jnp
from jax import lax
from jax.experimental import pallas as pl
from jax.experimental.pallas import tpu as pltpu
from jax.sharding import PartitionSpec as P

ITERS = 2
SPREAD = 10690

ridge_scale = 0.002


def squares(block):
    return jnp.sum(jnp.square(block.astype(jnp.float32)), axis=1)


def cross_piece(left, right):
    return lax.dot_general(
        left, right, (((1,), (1,)), ((), ())), preferred_element_type=jnp.float32
    )


def times(left, right, contract):
    return lax.dot_general(
        left, right, ((contract[:1], contract[1:]), ((), ())), precision=lax.Precision.HIGHEST
    )


NEIGHBOURS = [(0, 1), (1, 0), (2, 3), (3, 2)]


def handed(block):
    return lax.ppermute(block, "landmark", NEIGHBOURS)


def across(block):
    pairs = [(4 * p + z, 4 * p + 3 - z if z in (1, 2) else 4 * (p ^ 1) + z) for p in range(8) for z in range(4)]
    return lax.ppermute(block, ("proof", "landmark"), pairs)


def flipped(block, bits):
    return lax.ppermute(block, "proof", [(i, i ^ bits) for i in range(8)])


def sum_rows_axis(block):
    odd = lax.axis_index("proof") % 2
    half = block.shape[1] // 2
    low, high = block[:, :half], block[:, half:]
    return sum_halves(jnp.where(odd == 0, low, high), jnp.where(odd == 0, high, low))


def sum_halves(mine, other):
    odd = lax.axis_index("proof") % 2
    mine = mine + flipped(other, 1)
    mine = mine + flipped(mine, 2) + flipped(mine, 4) + flipped(mine, 6)
    other = flipped(mine, 1)
    low, high = jnp.where(odd == 0, mine, other), jnp.where(odd == 0, other, mine)
    return jnp.concatenate([low, high], axis=1)


def sum_middle(block):
    return block + across(block)


def packed(block, *vectors):
    rows = jnp.stack(vectors)
    rows = jnp.pad(rows, ((0, 8 - rows.shape[0]), (0, block.shape[1] - rows.shape[1])))
    return jnp.concatenate([block, rows], axis=0)


def after(block, *earlier):
    return lax.optimization_barrier((block, *earlier))[0]


ANY = pl.BlockSpec(memory_space=pltpu.HBM)
VMEM = pl.BlockSpec(memory_space=pltpu.VMEM)
SMEM = pl.BlockSpec(memory_space=pltpu.SMEM)


def place():
    return jnp.stack([lax.axis_index("proof"), lax.axis_index("landmark")]).astype(jnp.int32)


def add_squares(total_ref, block_ref, first=False):
    for r in range(0, block_ref.shape[0], 32):
        rows = slice(r, r + 32)
        total = None if first else total_ref[rows]
        for j in range(block_ref.shape[1] // 128):
            x = block_ref[rows, j * 128 : (j + 1) * 128].astype(jnp.float32)
            total = x * x if total is None else total + x * x
        total_ref[rows] = total


def across_lanes(norm_ref, inside):
    ones = jnp.ones((8, 128), jnp.float32)
    return lax.dot_general(ones, norm_ref[inside], (((1,), (1,)), ((), ())), precision=lax.Precision.HIGHEST)


def product(left, right):
    return lax.dot_general(left, right, (((1,), (1,)), ((), ())), preferred_element_type=jnp.float32)


def tiled_product(cross_ref, left, right_ref):
    for t in range(cross_ref.shape[0]):
        cross_ref[t] += product(left[...], right_ref[t * 256 : (t + 1) * 256])


def feature_block(z, zbits, side):
    return 2 * (z ^ zbits) + side


class Rows:
    def __init__(self, blocks):
        self.keys, self.blocks = list(blocks), list(blocks.values())

    def source(self, refs, zbits, side, width):
        if (zbits, None) in self.keys:
            return refs[self.keys.index((zbits, None))].at[:, pl.ds(side * width, width)]
        return refs[self.keys.index((zbits, side))]


class Landmarks:
    def __init__(self, parts):
        self.keys = [(bits, row) for bits, row, _ in parts]
        self.blocks = [block for _, _, block in parts]

    def start(self, refs, bits, target, sem):
        for (found, row), ref in zip(self.keys, refs):
            if found == bits:
                pltpu.make_async_copy(ref, target.at[pl.ds(row, ref.shape[0])], sem).start()

    def start_any(self, refs, bits, target, sem):
        for one in sorted({found for found, _ in self.keys}):
            @pl.when(bits == one)
            def _():
                self.start(refs, one, target, sem)


def wait(target, sem):
    pltpu.make_async_copy(target, target, sem).wait()


def call(body, inputs, specs, shapes, scratch, name):
    return pl.pallas_call(
        body,
        out_shape=tuple(jax.ShapeDtypeStruct(shape, jnp.float32) for shape in shapes),
        in_specs=specs,
        out_specs=tuple(VMEM for _ in shapes),
        scratch_shapes=scratch,
        compiler_params=pltpu.CompilerParams(vmem_limit_bytes=60 << 20),
        cost_estimate=pl.CostEstimate(flops=1000, bytes_accessed=1000, transcendentals=0),
        name=name,
    )(*inputs)


def own_block(rows, landmarks, n, m, width):
    rows, landmarks = Rows(rows), Landmarks(landmarks)
    sources = [(0, 0), (0, 1), (3, 0), (3, 1), (1, 0)]

    def body(place_ref, *refs):
        row_refs, refs = refs[: len(rows.keys)], refs[len(rows.keys) :]
        landmark_refs, refs = refs[: len(landmarks.keys)], refs[len(landmarks.keys) :]
        cross_ref, row_norm_ref, norm_ref, rows_s, land_s, norm_s, row_sem, land_sem = refs
        p, z = place_ref[0], place_ref[1]
        wanted = [feature_block(z, zbits, side) ^ p for zbits, side in sources]
        for i, (zbits, side) in enumerate(sources):
            pltpu.make_async_copy(rows.source(row_refs, zbits, side, width), rows_s.at[i], row_sem.at[i]).start()
        for bits in range(8):
            landmarks.start(landmark_refs, bits, land_s.at[bits], land_sem.at[bits])
        cross_ref[...] = jnp.zeros_like(cross_ref)
        for bits in range(8):
            wait(land_s.at[bits], land_sem.at[bits])
        for i in range(len(sources)):
            wait(rows_s.at[i], row_sem.at[i])
            tiled_product(cross_ref, rows_s.at[i], land_s.at[wanted[i]])
            add_squares(row_norm_ref, rows_s.at[i], first=i == 0)
            for bits in (2 * i, 2 * i + 1):
                if bits < 8:
                    add_squares(norm_s, land_s.at[bits], first=bits == 0)
        norm_ref[...] = across_lanes(norm_s, slice(None))

    return call(
        body,
        [place()] + rows.blocks + landmarks.blocks,
        [SMEM] + [ANY] * (len(rows.keys) + len(landmarks.keys)),
        [(m // 256, n, 256), (n, 128), (8, m)],
        [
            pltpu.VMEM((len(sources), n, width), jnp.bfloat16),
            pltpu.VMEM((8, m, width), jnp.bfloat16),
            pltpu.VMEM((m, 128), jnp.float32),
            pltpu.SemaphoreType.DMA((len(sources),)),
            pltpu.SemaphoreType.DMA((8,)),
        ],
        "own_block",
    )


def end_block(rows, own, end, cross_own, row_norm, n, m, width):
    rows, own, end = Rows(rows), Landmarks(own), Landmarks(end)
    late = 2 * 2 + 1

    def body(place_ref, cross_in, norm_in, *refs):
        row_refs, refs = refs[: len(rows.keys)], refs[len(rows.keys) :]
        own_refs, refs = refs[: len(own.keys)], refs[len(own.keys) :]
        end_refs, refs = refs[: len(end.keys)], refs[len(end.keys) :]
        cross_own_ref, cross_ref, row_norm_ref, norm_ref, rows_s, own_s, end_s, norm_s, row_sem, own_sem, end_sem, in_sem = refs
        p, z = place_ref[0], place_ref[1]
        more = [(1, 1), (2, 0)]
        carry = pltpu.make_async_copy(cross_in, cross_own_ref, in_sem)
        carry.start()
        for zbits, side in more:
            slot = 2 * zbits + side
            pltpu.make_async_copy(rows.source(row_refs, zbits, side, width), rows_s.at[slot], row_sem.at[slot]).start()
        for i, (zbits, side) in enumerate(more):
            own.start_any(own_refs, feature_block(z, zbits, side) ^ p, own_s.at[i], own_sem.at[i])
        for slot in range(8):
            if slot != late and (slot // 2, slot % 2) not in more:
                source = rows.source(row_refs, slot // 2, slot % 2, width)
                pltpu.make_async_copy(source, rows_s.at[slot], row_sem.at[slot]).start()
        for bits in range(6):
            end.start(end_refs, bits, end_s.at[bits], end_sem.at[bits])
        cross_ref[...] = jnp.zeros_like(cross_ref)
        rows_s[late] = jnp.zeros(rows_s.shape[1:], rows_s.dtype)
        row_norm_ref[...] = norm_in[...]
        carry.wait()
        for i, (zbits, side) in enumerate(more):
            slot = 2 * zbits + side
            wait(rows_s.at[slot], row_sem.at[slot])
            wait(own_s.at[i], own_sem.at[i])
            tiled_product(cross_own_ref, rows_s.at[slot], own_s.at[i])
            add_squares(row_norm_ref, rows_s.at[slot])
        for slot in range(8):
            if slot != late and (slot // 2, slot % 2) not in more:
                wait(rows_s.at[slot], row_sem.at[slot])
        for bits in range(6):
            wait(end_s.at[bits], end_sem.at[bits])
            f = p ^ bits
            slot = 2 * (z ^ (f // 2)) + f % 2
            tiled_product(cross_ref, rows_s.at[slot], end_s.at[bits])
            add_squares(norm_s, end_s.at[bits], first=bits == 0)
        norm_ref[...] = across_lanes(norm_s, slice(None))

    return call(
        body,
        [place(), cross_own, row_norm] + rows.blocks + own.blocks + end.blocks,
        [SMEM, ANY, VMEM] + [ANY] * (len(rows.keys) + len(own.keys) + len(end.keys)),
        [(m // 256, n, 256), (m // 256, n, 256), (n, 128), (8, m)],
        [
            pltpu.VMEM((8, n, width), jnp.bfloat16),
            pltpu.VMEM((2, m, width), jnp.bfloat16),
            pltpu.VMEM((6, m, width), jnp.bfloat16),
            pltpu.VMEM((m, 128), jnp.float32),
            pltpu.SemaphoreType.DMA((8,)),
            pltpu.SemaphoreType.DMA((2,)),
            pltpu.SemaphoreType.DMA((6,)),
            pltpu.SemaphoreType.DMA,
        ],
        "end_block",
    )


def last_block(rows, own, end, cross_own, cross_end, row_norm, norm_own, norm_end, columns, width):
    rows, own, end = Rows(rows), Landmarks(own), Landmarks(end)
    n, m, count = columns.shape[1], norm_own.shape[1], columns.shape[0]

    def body(place_ref, cross_own_in, cross_end_in, row_norm_in, norm_own_in, norm_end_in, columns_ref, *refs):
        row_refs, refs = refs[: len(rows.keys)], refs[len(rows.keys) :]
        own_refs, refs = refs[: len(own.keys)], refs[len(own.keys) :]
        end_refs, refs = refs[: len(end.keys)], refs[len(end.keys) :]
        kernel_ref, mine_ref, other_ref, *refs = refs
        cross_s, rows_s, own_s, end_s, row_norm_s, norm_s, sums_s, row_sem, own_sem, end_sem, in_sem = refs
        p, z = place_ref[0], place_ref[1]
        half = m // 256
        carry_own = pltpu.make_async_copy(cross_own_in, cross_s.at[:half], in_sem.at[0])
        carry_end = pltpu.make_async_copy(cross_end_in, cross_s.at[half:], in_sem.at[1])
        carry_own.start()
        carry_end.start()
        far = feature_block(z, 2, 1) ^ p
        pltpu.make_async_copy(rows.source(row_refs, 2, 1, width), rows_s.at[2], row_sem.at[2]).start()
        own.start_any(own_refs, far, own_s, own_sem)
        for i in range(2):
            f = p ^ (6 + i)
            for zbits in range(4):
                for side in range(2):
                    @pl.when((z ^ (f // 2) == zbits) & (f % 2 == side))
                    def _():
                        source = rows.source(row_refs, zbits, side, width)
                        pltpu.make_async_copy(source, rows_s.at[i], row_sem.at[i]).start()
            end.start(end_refs, 6 + i, end_s.at[i], end_sem.at[i])

        @pl.when(far < 6)
        def _():
            end.start_any(end_refs, far, end_s.at[2], end_sem.at[2])

        carry_own.wait()
        wait(rows_s.at[2], row_sem.at[2])
        wait(own_s, own_sem)
        tiled_product(cross_s.at[:half], rows_s.at[2], own_s)
        row_norm_s[...] = row_norm_in[...]
        add_squares(row_norm_s, rows_s.at[2])
        carry_end.wait()
        for i in range(2):
            wait(rows_s.at[i], row_sem.at[i])
            wait(end_s.at[i], end_sem.at[i])
            tiled_product(cross_s.at[half:], rows_s.at[i], end_s.at[i])
            add_squares(norm_s, end_s.at[i], first=i == 0)

        @pl.when(far < 6)
        def _():
            wait(end_s.at[2], end_sem.at[2])
            tiled_product(cross_s.at[half:], rows_s.at[2], end_s.at[2])

        row_norm = jnp.sum(row_norm_s[...], axis=1, keepdims=True)
        for t in range(2 * half):
            inside = slice(t * 256, (t + 1) * 256)
            if t < half:
                norm = norm_own_in[:1, inside]
            else:
                here = slice((t - half) * 256, (t - half + 1) * 256)
                norm = norm_end_in[:1, here] + across_lanes(norm_s, here)[:1]
            k = jnp.exp(-(row_norm + norm - 2.0 * cross_s[t]) / SPREAD)
            kernel_ref[:, inside] = k
            sums_s[:count, inside] = jnp.dot(columns_ref[...], k, precision=lax.Precision.HIGHEST)
            sums_s[count:, inside] = jnp.broadcast_to(jnp.sum(k * k, axis=0, keepdims=True), (8, 256))
        odd = p % 2 == 1
        mine_ref[...] = jnp.where(odd, sums_s[:, m:], sums_s[:, :m])
        other_ref[...] = jnp.where(odd, sums_s[:, :m], sums_s[:, m:])

    return call(
        body,
        [place(), cross_own, cross_end, row_norm, norm_own, norm_end, columns]
        + rows.blocks + own.blocks + end.blocks,
        [SMEM] + [ANY] * 2 + [VMEM] * 4 + [ANY] * (len(rows.keys) + len(own.keys) + len(end.keys)),
        [(n, 2 * m), (count + 8, m), (count + 8, m)],
        [
            pltpu.VMEM((2 * m // 256, n, 256), jnp.float32),
            pltpu.VMEM((3, n, width), jnp.bfloat16),
            pltpu.VMEM((m, width), jnp.bfloat16),
            pltpu.VMEM((3, m, width), jnp.bfloat16),
            pltpu.VMEM((n, 128), jnp.float32),
            pltpu.VMEM((m, 128), jnp.float32),
            pltpu.VMEM((count + 8, 2 * m), jnp.float32),
            pltpu.SemaphoreType.DMA((3,)),
            pltpu.SemaphoreType.DMA,
            pltpu.SemaphoreType.DMA((3,)),
            pltpu.SemaphoreType.DMA((2,)),
        ],
        "last_block",
    )


def middle_kernel(row_features, landmark_features, columns):
    own = landmark_features
    m, half = own.shape
    n, middle = row_features.shape[0], m // 2
    left, right = row_features[:, :half], row_features[:, half:]
    end = handed(own)
    own_x, own_y = flipped(own, 2), flipped(own, 4)
    middle_rows = across(row_features)
    own_x, own_y, end, left = lax.optimization_barrier((own_x, own_y, end, left))
    end_left = handed(left)
    own_low, own_high = flipped(own_x[:middle], 4), flipped(own_y[middle:], 2)
    other_own, other_x, other_y = flipped(after(own, own_x), 1), flipped(own_x, 1), flipped(own_y, 1)
    own_low, own_high, end = lax.optimization_barrier((own_low, own_high, end))
    end_x, end_y = flipped(end, 2), flipped(end, 4)
    other_low, other_high = flipped(own_low, 1), flipped(own_high, 1)
    end_bottom = end[middle:]
    end_left, right, middle_rows = lax.optimization_barrier((end_left, right, middle_rows))
    far_left = across(end_left)
    end_right = handed(right)
    own_parts = [
        (0, 0, own), (2, 0, own_x), (4, 0, own_y), (6, 0, own_low), (6, middle, own_high),
        (1, 0, other_own), (3, 0, other_x), (5, 0, other_y), (7, 0, other_low), (7, middle, other_high),
    ]
    rows = {(0, None): row_features, (3, None): middle_rows, (1, 0): end_left}
    cross_own, row_norm, norm_own = own_block(rows, own_parts, n, m, half)
    end_x, end_y, end_bottom, far_left, _ = lax.optimization_barrier((end_x, end_y, end_bottom, far_left, cross_own))
    end_high = flipped(end_bottom, 6)
    end_right = after(end_right, end_x, end_y)
    far_right = across(end_right)
    end_low = handed(after(own_low, end_right))
    end_parts = [(0, 0, end), (2, 0, end_x), (4, 0, end_y)]
    end_parts += [(bits + 1, row, flipped(block, 1)) for bits, row, block in end_parts]
    rows |= {(1, 1): end_right, (2, 0): far_left}
    cross_own, cross_end, row_norm, norm_end = end_block(
        rows, own_parts, end_parts, cross_own, row_norm, n, m, half
    )
    corner = [(6, 0, after(end_low, cross_end)), (6, middle, after(end_high, cross_end, far_right))]
    end_parts += corner + [(bits + 1, row, flipped(block, 1)) for bits, row, block in corner]
    rows |= {(2, 1): far_right}
    return last_block(
        rows, own_parts, end_parts, cross_own, cross_end, row_norm, norm_own, norm_end, columns, half
    )


def conjugate_gradients(kernel, sums, columns, lam, sum_rows, sum_landmarks):
    count = columns.shape[0]
    residual, precond = sums[:count], lam + sums[count]
    coefficient = jnp.zeros_like(residual)
    inner = None
    for iteration in range(ITERS):
        scaled = residual / precond
        part = times(scaled, kernel, (1, 1))
        dots = [jnp.sum(residual * scaled, axis=1), jnp.sum(scaled * scaled, axis=1)]
        if iteration > 0:
            dots.append(jnp.sum(scaled * direction, axis=1))
        sums = sum_landmarks(packed(part, *dots))
        inner_next, square = sums[count, :count], sums[count + 1, :count]
        if iteration == 0:
            direction, image, length = scaled, sums[:count], square
        else:
            beta = inner_next / inner
            length = square + beta * (2.0 * sums[count + 2, :count] + beta * length)
            direction = scaled + beta[:, None] * direction
            image = sums[:count] + beta[:, None] * image
        inner = inner_next
        sums = sum_rows(packed(times(image, kernel, (1, 0)), jnp.sum(image * image, axis=1)))
        gradient = sums[:count] + lam * direction
        step_size = (inner / (sums[count, :count] + lam * length))[:, None]
        coefficient = coefficient + step_size * direction
        residual = residual - step_size * gradient
    return coefficient, residual


def folded(row_features, landmark_features, targets):
    lam = ridge_scale * row_features.shape[0] * lax.axis_size("proof")
    columns = targets.T
    kernel, mine, other = middle_kernel(row_features, landmark_features, columns)
    sums = sum_halves(mine, other)
    coefficient, residual = conjugate_gradients(kernel, sums, columns, lam, sum_rows_axis, sum_middle)
    both = jnp.concatenate([coefficient, residual], axis=0)
    half = both.shape[1] // 2
    received = handed(both[:, half:])
    z = lax.axis_index("landmark")
    both = jnp.where((z == 1) | (z == 2), both[:, :half], received)
    return both[: columns.shape[0]].T, both[columns.shape[0] :].T


def plain(row_features, landmark_features, targets):
    lam = ridge_scale * row_features.shape[0] * lax.axis_size("proof")
    columns = targets.T
    rows = lax.all_gather(row_features, "landmark", axis=1, tiled=True)
    whole = lax.all_gather(landmark_features, "proof", axis=1, tiled=True)
    kernel = jnp.exp(-(squares(rows)[:, None] + squares(whole)[None, :] - 2.0 * cross_piece(rows, whole)) / SPREAD)
    sum_rows = lambda block: lax.psum(block, "proof")
    sums = sum_rows(packed(times(columns, kernel, (1, 0)), jnp.sum(kernel * kernel, axis=0)))
    sum_landmarks = lambda block: lax.psum(block, "landmark")
    coefficient, residual = conjugate_gradients(kernel, sums, columns, lam, sum_rows, sum_landmarks)
    return coefficient.T, residual.T


def solution(mesh):
    placed = (P("proof", "landmark"), P("landmark", "proof"), P("proof", None))
    four_planes = mesh.shape["proof"] == 8 and mesh.shape["landmark"] == 4
    return jax.shard_map(
        folded if four_planes else plain,
        mesh=mesh,
        in_specs=placed,
        out_specs=(P("landmark", None), P("landmark", None)),
        check_vma=False,
    )
```

```python
import jax
import jax.numpy as jnp
from jax import lax
from jax.experimental import pallas as pl
from jax.experimental.pallas import tpu as pltpu
from jax.sharding import PartitionSpec as P

ITERS = 2
SPREAD = 10690

ridge_scale = 0.002


def squares(block):
    return jnp.sum(jnp.square(block.astype(jnp.float32)), axis=1)


def cross_piece(left, right):
    return lax.dot_general(
        left, right, (((1,), (1,)), ((), ())), preferred_element_type=jnp.float32
    )


def times(left, right, contract):
    return lax.dot_general(
        left, right, ((contract[:1], contract[1:]), ((), ())), precision=lax.Precision.HIGHEST
    )


NEIGHBOURS = [(0, 1), (1, 0), (2, 3), (3, 2)]


def handed(block):
    return lax.ppermute(block, "landmark", NEIGHBOURS)


def across(block):
    pairs = [(4 * p + z, 4 * p + 3 - z if z in (1, 2) else 4 * (p ^ 1) + z) for p in range(8) for z in range(4)]
    return lax.ppermute(block, ("proof", "landmark"), pairs)


def flipped(block, bits):
    return lax.ppermute(block, "proof", [(i, i ^ bits) for i in range(8)])


def sum_rows_axis(block):
    odd = lax.axis_index("proof") % 2
    half = block.shape[1] // 2
    low, high = block[:, :half], block[:, half:]
    return sum_halves(jnp.where(odd == 0, low, high), jnp.where(odd == 0, high, low))


def sum_halves(mine, other):
    odd = lax.axis_index("proof") % 2
    mine = mine + flipped(other, 1)
    mine = mine + flipped(mine, 2) + flipped(mine, 4) + flipped(mine, 6)
    other = flipped(mine, 1)
    low, high = jnp.where(odd == 0, mine, other), jnp.where(odd == 0, other, mine)
    return jnp.concatenate([low, high], axis=1)


def sum_middle(block):
    return block + across(block)


def packed(block, *vectors):
    rows = jnp.stack(vectors)
    rows = jnp.pad(rows, ((0, 8 - rows.shape[0]), (0, block.shape[1] - rows.shape[1])))
    return jnp.concatenate([block, rows], axis=0)


def after(block, *earlier):
    return lax.optimization_barrier((block, *earlier))[0]


ANY = pl.BlockSpec(memory_space=pltpu.HBM)
VMEM = pl.BlockSpec(memory_space=pltpu.VMEM)
SMEM = pl.BlockSpec(memory_space=pltpu.SMEM)


def place():
    return jnp.stack([lax.axis_index("proof"), lax.axis_index("landmark")]).astype(jnp.int32)


def add_squares(total_ref, block_ref, first=False):
    for r in range(0, block_ref.shape[0], 32):
        rows = slice(r, r + 32)
        total = None if first else total_ref[rows]
        for j in range(block_ref.shape[1] // 128):
            x = block_ref[rows, j * 128 : (j + 1) * 128].astype(jnp.float32)
            total = x * x if total is None else total + x * x
        total_ref[rows] = total


def across_lanes(norm_ref, inside):
    ones = jnp.ones((8, 128), jnp.float32)
    return lax.dot_general(ones, norm_ref[inside], (((1,), (1,)), ((), ())), precision=lax.Precision.HIGHEST)


def product(left, right):
    return lax.dot_general(left, right, (((1,), (1,)), ((), ())), preferred_element_type=jnp.float32)


def tiled_product(cross_ref, left, right_ref):
    for t in range(cross_ref.shape[0]):
        cross_ref[t] += product(left[...], right_ref[t * 256 : (t + 1) * 256])


def feature_block(z, zbits, side):
    return 2 * (z ^ zbits) + side


class Rows:
    def __init__(self, blocks):
        self.keys, self.blocks = list(blocks), list(blocks.values())

    def source(self, refs, zbits, side, width):
        if (zbits, None) in self.keys:
            return refs[self.keys.index((zbits, None))].at[:, pl.ds(side * width, width)]
        return refs[self.keys.index((zbits, side))]


class Landmarks:
    def __init__(self, parts):
        self.keys = [(bits, row) for bits, row, _ in parts]
        self.blocks = [block for _, _, block in parts]

    def start(self, refs, bits, target, sem):
        for (found, row), ref in zip(self.keys, refs):
            if found == bits:
                pltpu.make_async_copy(ref, target.at[pl.ds(row, ref.shape[0])], sem).start()

    def start_any(self, refs, bits, target, sem):
        for one in sorted({found for found, _ in self.keys}):
            @pl.when(bits == one)
            def _():
                self.start(refs, one, target, sem)


def wait(target, sem):
    pltpu.make_async_copy(target, target, sem).wait()


def call(body, inputs, specs, shapes, scratch, name):
    return pl.pallas_call(
        body,
        out_shape=tuple(jax.ShapeDtypeStruct(shape, jnp.float32) for shape in shapes),
        in_specs=specs,
        out_specs=tuple(VMEM for _ in shapes),
        scratch_shapes=scratch,
        compiler_params=pltpu.CompilerParams(vmem_limit_bytes=60 << 20),
        cost_estimate=pl.CostEstimate(flops=1000, bytes_accessed=1000, transcendentals=0),
        name=name,
    )(*inputs)


def own_block(rows, landmarks, n, m, width):
    rows, landmarks = Rows(rows), Landmarks(landmarks)
    sources = [(0, 0), (0, 1), (3, 0), (3, 1), (1, 0)]

    def body(place_ref, *refs):
        row_refs, refs = refs[: len(rows.keys)], refs[len(rows.keys) :]
        landmark_refs, refs = refs[: len(landmarks.keys)], refs[len(landmarks.keys) :]
        cross_ref, row_norm_ref, norm_ref, rows_s, land_s, norm_s, row_sem, land_sem = refs
        p, z = place_ref[0], place_ref[1]
        wanted = [feature_block(z, zbits, side) ^ p for zbits, side in sources]
        for i, (zbits, side) in enumerate(sources):
            pltpu.make_async_copy(rows.source(row_refs, zbits, side, width), rows_s.at[i], row_sem.at[i]).start()
        for bits in range(8):
            landmarks.start(landmark_refs, bits, land_s.at[bits], land_sem.at[bits])
        cross_ref[...] = jnp.zeros_like(cross_ref)
        for bits in range(8):
            wait(land_s.at[bits], land_sem.at[bits])
        for i in range(len(sources)):
            wait(rows_s.at[i], row_sem.at[i])
            tiled_product(cross_ref, rows_s.at[i], land_s.at[wanted[i]])
            add_squares(row_norm_ref, rows_s.at[i], first=i == 0)
            for bits in (2 * i, 2 * i + 1):
                if bits < 8:
                    add_squares(norm_s, land_s.at[bits], first=bits == 0)
        norm_ref[...] = across_lanes(norm_s, slice(None))

    return call(
        body,
        [place()] + rows.blocks + landmarks.blocks,
        [SMEM] + [ANY] * (len(rows.keys) + len(landmarks.keys)),
        [(m // 256, n, 256), (n, 128), (8, m)],
        [
            pltpu.VMEM((len(sources), n, width), jnp.bfloat16),
            pltpu.VMEM((8, m, width), jnp.bfloat16),
            pltpu.VMEM((m, 128), jnp.float32),
            pltpu.SemaphoreType.DMA((len(sources),)),
            pltpu.SemaphoreType.DMA((8,)),
        ],
        "own_block",
    )


def end_block(rows, own, end, cross_own, row_norm, n, m, width):
    rows, own, end = Rows(rows), Landmarks(own), Landmarks(end)
    late = 2 * 2 + 1

    def body(place_ref, cross_in, norm_in, *refs):
        row_refs, refs = refs[: len(rows.keys)], refs[len(rows.keys) :]
        own_refs, refs = refs[: len(own.keys)], refs[len(own.keys) :]
        end_refs, refs = refs[: len(end.keys)], refs[len(end.keys) :]
        cross_own_ref, cross_ref, row_norm_ref, norm_ref, rows_s, own_s, end_s, norm_s, row_sem, own_sem, end_sem, in_sem = refs
        p, z = place_ref[0], place_ref[1]
        more = [(1, 1), (2, 0)]
        carry = pltpu.make_async_copy(cross_in, cross_own_ref, in_sem)
        carry.start()
        for zbits, side in more:
            slot = 2 * zbits + side
            pltpu.make_async_copy(rows.source(row_refs, zbits, side, width), rows_s.at[slot], row_sem.at[slot]).start()
        for i, (zbits, side) in enumerate(more):
            own.start_any(own_refs, feature_block(z, zbits, side) ^ p, own_s.at[i], own_sem.at[i])
        for slot in range(8):
            if slot != late and (slot // 2, slot % 2) not in more:
                source = rows.source(row_refs, slot // 2, slot % 2, width)
                pltpu.make_async_copy(source, rows_s.at[slot], row_sem.at[slot]).start()
        for bits in range(6):
            end.start(end_refs, bits, end_s.at[bits], end_sem.at[bits])
        cross_ref[...] = jnp.zeros_like(cross_ref)
        rows_s[late] = jnp.zeros(rows_s.shape[1:], rows_s.dtype)
        row_norm_ref[...] = norm_in[...]
        carry.wait()
        for i, (zbits, side) in enumerate(more):
            slot = 2 * zbits + side
            wait(rows_s.at[slot], row_sem.at[slot])
            wait(own_s.at[i], own_sem.at[i])
            tiled_product(cross_own_ref, rows_s.at[slot], own_s.at[i])
            add_squares(row_norm_ref, rows_s.at[slot])
        for slot in range(8):
            if slot != late and (slot // 2, slot % 2) not in more:
                wait(rows_s.at[slot], row_sem.at[slot])
        for bits in range(6):
            wait(end_s.at[bits], end_sem.at[bits])
            f = p ^ bits
            slot = 2 * (z ^ (f // 2)) + f % 2
            tiled_product(cross_ref, rows_s.at[slot], end_s.at[bits])
            add_squares(norm_s, end_s.at[bits], first=bits == 0)
        norm_ref[...] = across_lanes(norm_s, slice(None))

    return call(
        body,
        [place(), cross_own, row_norm] + rows.blocks + own.blocks + end.blocks,
        [SMEM, ANY, VMEM] + [ANY] * (len(rows.keys) + len(own.keys) + len(end.keys)),
        [(m // 256, n, 256), (m // 256, n, 256), (n, 128), (8, m)],
        [
            pltpu.VMEM((8, n, width), jnp.bfloat16),
            pltpu.VMEM((2, m, width), jnp.bfloat16),
            pltpu.VMEM((6, m, width), jnp.bfloat16),
            pltpu.VMEM((m, 128), jnp.float32),
            pltpu.SemaphoreType.DMA((8,)),
            pltpu.SemaphoreType.DMA((2,)),
            pltpu.SemaphoreType.DMA((6,)),
            pltpu.SemaphoreType.DMA,
        ],
        "end_block",
    )


def last_block(rows, own, end, cross_own, cross_end, row_norm, norm_own, norm_end, columns, width):
    rows, own, end = Rows(rows), Landmarks(own), Landmarks(end)
    n, m, count = columns.shape[1], norm_own.shape[1], columns.shape[0]

    def body(place_ref, cross_own_in, cross_end_in, row_norm_in, norm_own_in, norm_end_in, columns_ref, *refs):
        row_refs, refs = refs[: len(rows.keys)], refs[len(rows.keys) :]
        own_refs, refs = refs[: len(own.keys)], refs[len(own.keys) :]
        end_refs, refs = refs[: len(end.keys)], refs[len(end.keys) :]
        kernel_ref, mine_ref, other_ref, *refs = refs
        cross_s, rows_s, own_s, end_s, row_norm_s, norm_s, sums_s, row_sem, own_sem, end_sem, in_sem = refs
        p, z = place_ref[0], place_ref[1]
        half = m // 256
        carry_own = pltpu.make_async_copy(cross_own_in, cross_s.at[:half], in_sem.at[0])
        carry_end = pltpu.make_async_copy(cross_end_in, cross_s.at[half:], in_sem.at[1])
        carry_own.start()
        carry_end.start()
        far = feature_block(z, 2, 1) ^ p
        pltpu.make_async_copy(rows.source(row_refs, 2, 1, width), rows_s.at[2], row_sem.at[2]).start()
        own.start_any(own_refs, far, own_s, own_sem)
        for i in range(2):
            f = p ^ (6 + i)
            for zbits in range(4):
                for side in range(2):
                    @pl.when((z ^ (f // 2) == zbits) & (f % 2 == side))
                    def _():
                        source = rows.source(row_refs, zbits, side, width)
                        pltpu.make_async_copy(source, rows_s.at[i], row_sem.at[i]).start()
            end.start(end_refs, 6 + i, end_s.at[i], end_sem.at[i])

        @pl.when(far < 6)
        def _():
            end.start_any(end_refs, far, end_s.at[2], end_sem.at[2])

        carry_own.wait()
        wait(rows_s.at[2], row_sem.at[2])
        wait(own_s, own_sem)
        tiled_product(cross_s.at[:half], rows_s.at[2], own_s)
        row_norm_s[...] = row_norm_in[...]
        add_squares(row_norm_s, rows_s.at[2])
        carry_end.wait()
        for i in range(2):
            wait(rows_s.at[i], row_sem.at[i])
            wait(end_s.at[i], end_sem.at[i])
            tiled_product(cross_s.at[half:], rows_s.at[i], end_s.at[i])
            add_squares(norm_s, end_s.at[i], first=i == 0)

        @pl.when(far < 6)
        def _():
            wait(end_s.at[2], end_sem.at[2])
            tiled_product(cross_s.at[half:], rows_s.at[2], end_s.at[2])

        row_norm = jnp.sum(row_norm_s[...], axis=1, keepdims=True)
        for t in range(2 * half):
            inside = slice(t * 256, (t + 1) * 256)
            if t < half:
                norm = norm_own_in[:1, inside]
            else:
                here = slice((t - half) * 256, (t - half + 1) * 256)
                norm = norm_end_in[:1, here] + across_lanes(norm_s, here)[:1]
            k = jnp.exp(-(row_norm + norm - 2.0 * cross_s[t]) / SPREAD)
            kernel_ref[:, inside] = k
            sums_s[:count, inside] = jnp.dot(columns_ref[...], k, precision=lax.Precision.HIGHEST)
            sums_s[count:, inside] = jnp.broadcast_to(jnp.sum(k * k, axis=0, keepdims=True), (8, 256))
        odd = p % 2 == 1
        mine_ref[...] = jnp.where(odd, sums_s[:, m:], sums_s[:, :m])
        other_ref[...] = jnp.where(odd, sums_s[:, :m], sums_s[:, m:])

    return call(
        body,
        [place(), cross_own, cross_end, row_norm, norm_own, norm_end, columns]
        + rows.blocks + own.blocks + end.blocks,
        [SMEM] + [ANY] * 2 + [VMEM] * 4 + [ANY] * (len(rows.keys) + len(own.keys) + len(end.keys)),
        [(n, 2 * m), (count + 8, m), (count + 8, m)],
        [
            pltpu.VMEM((2 * m // 256, n, 256), jnp.float32),
            pltpu.VMEM((3, n, width), jnp.bfloat16),
            pltpu.VMEM((m, width), jnp.bfloat16),
            pltpu.VMEM((3, m, width), jnp.bfloat16),
            pltpu.VMEM((n, 128), jnp.float32),
            pltpu.VMEM((m, 128), jnp.float32),
            pltpu.VMEM((count + 8, 2 * m), jnp.float32),
            pltpu.SemaphoreType.DMA((3,)),
            pltpu.SemaphoreType.DMA,
            pltpu.SemaphoreType.DMA((3,)),
            pltpu.SemaphoreType.DMA((2,)),
        ],
        "last_block",
    )


def middle_kernel(row_features, landmark_features, columns):
    own = landmark_features
    m, half = own.shape
    n, middle = row_features.shape[0], m // 2
    left, right = row_features[:, :half], row_features[:, half:]
    end = handed(own)
    own_x, own_y = flipped(own, 2), flipped(own, 4)
    middle_rows = across(row_features)
    own_x, own_y, end, left = lax.optimization_barrier((own_x, own_y, end, left))
    end_left = handed(left)
    own_low, own_high = flipped(own_x[:middle], 4), flipped(own_y[middle:], 2)
    other_own, other_x, other_y = flipped(after(own, own_x), 1), flipped(own_x, 1), flipped(own_y, 1)
    own_low, own_high, end = lax.optimization_barrier((own_low, own_high, end))
    end_x, end_y = flipped(end, 2), flipped(end, 4)
    other_low, other_high = flipped(own_low, 1), flipped(own_high, 1)
    end_bottom = end[middle:]
    end_left, right, middle_rows = lax.optimization_barrier((end_left, right, middle_rows))
    far_left = across(end_left)
    end_right = handed(right)
    own_parts = [
        (0, 0, own), (2, 0, own_x), (4, 0, own_y), (6, 0, own_low), (6, middle, own_high),
        (1, 0, other_own), (3, 0, other_x), (5, 0, other_y), (7, 0, other_low), (7, middle, other_high),
    ]
    rows = {(0, None): row_features, (3, None): middle_rows, (1, 0): end_left}
    cross_own, row_norm, norm_own = own_block(rows, own_parts, n, m, half)
    end_x, end_y, end_bottom, far_left, _ = lax.optimization_barrier((end_x, end_y, end_bottom, far_left, cross_own))
    end_high = flipped(end_bottom, 6)
    end_right = after(end_right, end_x, end_y)
    far_right = across(end_right)
    end_low = handed(after(own_low, end_right))
    end_parts = [(0, 0, end), (2, 0, end_x), (4, 0, end_y)]
    end_parts += [(bits + 1, row, flipped(block, 1)) for bits, row, block in end_parts]
    rows |= {(1, 1): end_right, (2, 0): far_left}
    cross_own, cross_end, row_norm, norm_end = end_block(
        rows, own_parts, end_parts, cross_own, row_norm, n, m, half
    )
    corner = [(6, 0, after(end_low, cross_end)), (6, middle, after(end_high, cross_end, far_right))]
    end_parts += corner + [(bits + 1, row, flipped(block, 1)) for bits, row, block in corner]
    rows |= {(2, 1): far_right}
    return last_block(
        rows, own_parts, end_parts, cross_own, cross_end, row_norm, norm_own, norm_end, columns, half
    )


def conjugate_gradients(kernel, sums, columns, lam, sum_rows, sum_landmarks, settle=None):
    count = columns.shape[0]
    residual, precond = sums[:count], lam + sums[count]
    coefficient = jnp.zeros_like(residual)
    inner = None
    for iteration in range(ITERS):
        scaled = residual / precond
        part = times(scaled, kernel, (1, 1))
        dots = [jnp.sum(residual * scaled, axis=1), jnp.sum(scaled * scaled, axis=1)]
        if iteration > 0:
            dots.append(jnp.sum(scaled * direction, axis=1))
        sums = sum_landmarks(packed(part, *dots))
        inner_next, square = sums[count, :count], sums[count + 1, :count]
        if iteration == 0:
            direction, image, length = scaled, sums[:count], square
        else:
            beta = inner_next / inner
            length = square + beta * (2.0 * sums[count + 2, :count] + beta * length)
            direction = scaled + beta[:, None] * direction
            image = sums[:count] + beta[:, None] * image
        inner = inner_next
        last = packed(times(image, kernel, (1, 0)), jnp.sum(image * image, axis=1))
        if settle is not None and iteration == ITERS - 1:
            state, finish = settle((coefficient, residual, direction), packed_twice((inner, lam * length), last.shape[1]))
            sums = finish(sum_rows(last.at[count:].set(packed_twice((jnp.sum(image * image, axis=1),), last.shape[1]))))
            coefficient, residual, direction = (state[i * count : (i + 1) * count] for i in range(3))
            inner, ridge = state[3 * count, :count], state[3 * count + 1, :count]
        else:
            sums = sum_rows(last)
            ridge = lam * length
        gradient = sums[:count] + lam * direction
        step_size = (inner / (sums[count, :count] + ridge))[:, None]
        coefficient = coefficient + step_size * direction
        residual = residual - step_size * gradient
    return coefficient, residual


def packed_twice(vectors, width):
    rows = jnp.stack(vectors)
    rows = jnp.pad(rows, ((0, 8 - rows.shape[0]), (0, width // 2 - rows.shape[1])))
    return jnp.concatenate([rows, rows], axis=1)


def settled(state, vectors):
    z = lax.axis_index("landmark")
    middle = (z == 1) | (z == 2)
    whole = jnp.concatenate([*state, vectors], axis=0)
    half = whole.shape[1] // 2
    taken = jnp.where(middle, whole[:, :half], handed(whole[:, half:]))

    def finish(sums):
        return jnp.where(middle, sums[:, :half], handed(sums[:, half:]))

    return taken, finish


def folded(row_features, landmark_features, targets):
    lam = ridge_scale * row_features.shape[0] * lax.axis_size("proof")
    columns = targets.T
    kernel, mine, other = middle_kernel(row_features, landmark_features, columns)
    sums = sum_halves(mine, other)
    coefficient, residual = conjugate_gradients(kernel, sums, columns, lam, sum_rows_axis, sum_middle, settled)
    return coefficient.T, residual.T


def plain(row_features, landmark_features, targets):
    lam = ridge_scale * row_features.shape[0] * lax.axis_size("proof")
    columns = targets.T
    rows = lax.all_gather(row_features, "landmark", axis=1, tiled=True)
    whole = lax.all_gather(landmark_features, "proof", axis=1, tiled=True)
    kernel = jnp.exp(-(squares(rows)[:, None] + squares(whole)[None, :] - 2.0 * cross_piece(rows, whole)) / SPREAD)
    sum_rows = lambda block: lax.psum(block, "proof")
    sums = sum_rows(packed(times(columns, kernel, (1, 0)), jnp.sum(kernel * kernel, axis=0)))
    sum_landmarks = lambda block: lax.psum(block, "landmark")
    coefficient, residual = conjugate_gradients(kernel, sums, columns, lam, sum_rows, sum_landmarks)
    return coefficient.T, residual.T


def solution(mesh):
    placed = (P("proof", "landmark"), P("landmark", "proof"), P("proof", None))
    four_planes = mesh.shape["proof"] == 8 and mesh.shape["landmark"] == 4
    return jax.shard_map(
        folded if four_planes else plain,
        mesh=mesh,
        in_specs=placed,
        out_specs=(P("landmark", None), P("landmark", None)),
        check_vma=False,
    )
```

```python
import jax
import jax.numpy as jnp
from jax import lax
from jax.experimental import pallas as pl
from jax.experimental.pallas import tpu as pltpu
from jax.sharding import PartitionSpec as P

ITERS = 2
SPREAD = 10690

ridge_scale = 0.002


def squares(block):
    return jnp.sum(jnp.square(block.astype(jnp.float32)), axis=1)


def cross_piece(left, right):
    return lax.dot_general(
        left, right, (((1,), (1,)), ((), ())), preferred_element_type=jnp.float32
    )


def times(left, right, contract):
    return lax.dot_general(
        left, right, ((contract[:1], contract[1:]), ((), ())), precision=lax.Precision.HIGHEST
    )


NEIGHBOURS = [(0, 1), (1, 0), (2, 3), (3, 2)]


def handed(block):
    return lax.ppermute(block, "landmark", NEIGHBOURS)


def across(block):
    pairs = [(4 * p + z, 4 * p + 3 - z if z in (1, 2) else 4 * (p ^ 1) + z) for p in range(8) for z in range(4)]
    return lax.ppermute(block, ("proof", "landmark"), pairs)


def flipped(block, bits):
    return lax.ppermute(block, "proof", [(i, i ^ bits) for i in range(8)])


def sum_rows_axis(block):
    odd = lax.axis_index("proof") % 2
    half = block.shape[1] // 2
    low, high = block[:, :half], block[:, half:]
    return sum_halves(jnp.where(odd == 0, low, high), jnp.where(odd == 0, high, low))


def sum_halves(mine, other):
    odd = lax.axis_index("proof") % 2
    mine = mine + flipped(other, 1)
    mine = mine + flipped(mine, 2) + flipped(mine, 4) + flipped(mine, 6)
    other = flipped(mine, 1)
    low, high = jnp.where(odd == 0, mine, other), jnp.where(odd == 0, other, mine)
    return jnp.concatenate([low, high], axis=1)


def sum_middle(block):
    return block + across(block)


def packed(block, *vectors):
    rows = jnp.stack(vectors)
    rows = jnp.pad(rows, ((0, 8 - rows.shape[0]), (0, block.shape[1] - rows.shape[1])))
    return jnp.concatenate([block, rows], axis=0)


def after(block, *earlier):
    return lax.optimization_barrier((block, *earlier))[0]


ANY = pl.BlockSpec(memory_space=pltpu.HBM)
VMEM = pl.BlockSpec(memory_space=pltpu.VMEM)
SMEM = pl.BlockSpec(memory_space=pltpu.SMEM)


def place():
    return jnp.stack([lax.axis_index("proof"), lax.axis_index("landmark")]).astype(jnp.int32)


def add_squares(total_ref, block_ref, first=False):
    for r in range(0, block_ref.shape[0], 32):
        rows = slice(r, r + 32)
        total = None if first else total_ref[rows]
        for j in range(block_ref.shape[1] // 128):
            x = block_ref[rows, j * 128 : (j + 1) * 128].astype(jnp.float32)
            total = x * x if total is None else total + x * x
        total_ref[rows] = total


def across_lanes(norm_ref, inside):
    ones = jnp.ones((8, 128), jnp.float32)
    return lax.dot_general(ones, norm_ref[inside], (((1,), (1,)), ((), ())), precision=lax.Precision.HIGHEST)


def product(left, right):
    return lax.dot_general(left, right, (((1,), (1,)), ((), ())), preferred_element_type=jnp.float32)


def tiled_product(cross_ref, left, right_ref):
    for t in range(cross_ref.shape[0]):
        cross_ref[t] += product(left[...], right_ref[t * 256 : (t + 1) * 256])


def feature_block(z, zbits, side):
    return 2 * (z ^ zbits) + side


class Rows:
    def __init__(self, blocks):
        self.keys, self.blocks = list(blocks), list(blocks.values())

    def source(self, refs, zbits, side, width):
        if (zbits, None) in self.keys:
            return refs[self.keys.index((zbits, None))].at[:, pl.ds(side * width, width)]
        return refs[self.keys.index((zbits, side))]


class Landmarks:
    def __init__(self, parts):
        self.keys = [(bits, row) for bits, row, _ in parts]
        self.blocks = [block for _, _, block in parts]

    def start(self, refs, bits, target, sem):
        for (found, row), ref in zip(self.keys, refs):
            if found == bits:
                pltpu.make_async_copy(ref, target.at[pl.ds(row, ref.shape[0])], sem).start()

    def start_any(self, refs, bits, target, sem):
        for one in sorted({found for found, _ in self.keys}):
            @pl.when(bits == one)
            def _():
                self.start(refs, one, target, sem)


def wait(target, sem):
    pltpu.make_async_copy(target, target, sem).wait()


def call(body, inputs, specs, shapes, scratch, name):
    return pl.pallas_call(
        body,
        out_shape=tuple(jax.ShapeDtypeStruct(shape, jnp.float32) for shape in shapes),
        in_specs=specs,
        out_specs=tuple(VMEM for _ in shapes),
        scratch_shapes=scratch,
        compiler_params=pltpu.CompilerParams(vmem_limit_bytes=60 << 20),
        cost_estimate=pl.CostEstimate(flops=1000, bytes_accessed=1000, transcendentals=0),
        name=name,
    )(*inputs)


def own_block(rows, landmarks, n, m, width):
    rows, landmarks = Rows(rows), Landmarks(landmarks)
    sources = [(0, 0), (0, 1), (3, 0), (3, 1), (1, 0)]

    def body(place_ref, *refs):
        row_refs, refs = refs[: len(rows.keys)], refs[len(rows.keys) :]
        landmark_refs, refs = refs[: len(landmarks.keys)], refs[len(landmarks.keys) :]
        cross_ref, row_norm_ref, norm_ref, rows_s, land_s, norm_s, row_sem, land_sem = refs
        p, z = place_ref[0], place_ref[1]
        wanted = [feature_block(z, zbits, side) ^ p for zbits, side in sources]
        for i, (zbits, side) in enumerate(sources):
            pltpu.make_async_copy(rows.source(row_refs, zbits, side, width), rows_s.at[i], row_sem.at[i]).start()
        for bits in range(8):
            landmarks.start(landmark_refs, bits, land_s.at[bits], land_sem.at[bits])
        cross_ref[...] = jnp.zeros_like(cross_ref)
        for bits in range(8):
            wait(land_s.at[bits], land_sem.at[bits])
        for i in range(len(sources)):
            wait(rows_s.at[i], row_sem.at[i])
            tiled_product(cross_ref, rows_s.at[i], land_s.at[wanted[i]])
            add_squares(row_norm_ref, rows_s.at[i], first=i == 0)
            for bits in (2 * i, 2 * i + 1):
                if bits < 8:
                    add_squares(norm_s, land_s.at[bits], first=bits == 0)
        norm_ref[...] = across_lanes(norm_s, slice(None))

    return call(
        body,
        [place()] + rows.blocks + landmarks.blocks,
        [SMEM] + [ANY] * (len(rows.keys) + len(landmarks.keys)),
        [(m // 256, n, 256), (n, 128), (8, m)],
        [
            pltpu.VMEM((len(sources), n, width), jnp.bfloat16),
            pltpu.VMEM((8, m, width), jnp.bfloat16),
            pltpu.VMEM((m, 128), jnp.float32),
            pltpu.SemaphoreType.DMA((len(sources),)),
            pltpu.SemaphoreType.DMA((8,)),
        ],
        "own_block",
    )


def end_block(rows, own, end, cross_own, row_norm, n, m, width):
    rows, own, end = Rows(rows), Landmarks(own), Landmarks(end)
    late = 2 * 2 + 1

    def body(place_ref, cross_in, norm_in, *refs):
        row_refs, refs = refs[: len(rows.keys)], refs[len(rows.keys) :]
        own_refs, refs = refs[: len(own.keys)], refs[len(own.keys) :]
        end_refs, refs = refs[: len(end.keys)], refs[len(end.keys) :]
        cross_own_ref, cross_ref, row_norm_ref, norm_ref, rows_s, own_s, end_s, norm_s, row_sem, own_sem, end_sem, in_sem = refs
        p, z = place_ref[0], place_ref[1]
        more = [(1, 1), (2, 0)]
        carry = pltpu.make_async_copy(cross_in, cross_own_ref, in_sem)
        carry.start()
        for zbits, side in more:
            slot = 2 * zbits + side
            pltpu.make_async_copy(rows.source(row_refs, zbits, side, width), rows_s.at[slot], row_sem.at[slot]).start()
        for i, (zbits, side) in enumerate(more):
            own.start_any(own_refs, feature_block(z, zbits, side) ^ p, own_s.at[i], own_sem.at[i])
        for slot in range(8):
            if slot != late and (slot // 2, slot % 2) not in more:
                source = rows.source(row_refs, slot // 2, slot % 2, width)
                pltpu.make_async_copy(source, rows_s.at[slot], row_sem.at[slot]).start()
        for bits in range(6):
            end.start(end_refs, bits, end_s.at[bits], end_sem.at[bits])
        cross_ref[...] = jnp.zeros_like(cross_ref)
        rows_s[late] = jnp.zeros(rows_s.shape[1:], rows_s.dtype)
        row_norm_ref[...] = norm_in[...]
        carry.wait()
        for i, (zbits, side) in enumerate(more):
            slot = 2 * zbits + side
            wait(rows_s.at[slot], row_sem.at[slot])
            wait(own_s.at[i], own_sem.at[i])
            tiled_product(cross_own_ref, rows_s.at[slot], own_s.at[i])
            add_squares(row_norm_ref, rows_s.at[slot])
        for slot in range(8):
            if slot != late and (slot // 2, slot % 2) not in more:
                wait(rows_s.at[slot], row_sem.at[slot])
        for bits in range(6):
            wait(end_s.at[bits], end_sem.at[bits])
            f = p ^ bits
            slot = 2 * (z ^ (f // 2)) + f % 2
            tiled_product(cross_ref, rows_s.at[slot], end_s.at[bits])
            add_squares(norm_s, end_s.at[bits], first=bits == 0)
        norm_ref[...] = across_lanes(norm_s, slice(None))

    return call(
        body,
        [place(), cross_own, row_norm] + rows.blocks + own.blocks + end.blocks,
        [SMEM, ANY, VMEM] + [ANY] * (len(rows.keys) + len(own.keys) + len(end.keys)),
        [(m // 256, n, 256), (m // 256, n, 256), (n, 128), (8, m)],
        [
            pltpu.VMEM((8, n, width), jnp.bfloat16),
            pltpu.VMEM((2, m, width), jnp.bfloat16),
            pltpu.VMEM((6, m, width), jnp.bfloat16),
            pltpu.VMEM((m, 128), jnp.float32),
            pltpu.SemaphoreType.DMA((8,)),
            pltpu.SemaphoreType.DMA((2,)),
            pltpu.SemaphoreType.DMA((6,)),
            pltpu.SemaphoreType.DMA,
        ],
        "end_block",
    )


def last_block(rows, own, end, cross_own, cross_end, row_norm, norm_own, norm_end, columns, width):
    rows, own, end = Rows(rows), Landmarks(own), Landmarks(end)
    n, m, count = columns.shape[1], norm_own.shape[1], columns.shape[0]

    def body(place_ref, cross_own_in, cross_end_in, row_norm_in, norm_own_in, norm_end_in, columns_ref, *refs):
        row_refs, refs = refs[: len(rows.keys)], refs[len(rows.keys) :]
        own_refs, refs = refs[: len(own.keys)], refs[len(own.keys) :]
        end_refs, refs = refs[: len(end.keys)], refs[len(end.keys) :]
        kernel_ref, mine_ref, other_ref, *refs = refs
        cross_s, rows_s, own_s, end_s, row_norm_s, norm_s, sums_s, row_sem, own_sem, end_sem, in_sem = refs
        p, z = place_ref[0], place_ref[1]
        half = m // 256
        carry_own = pltpu.make_async_copy(cross_own_in, cross_s.at[:half], in_sem.at[0])
        carry_end = pltpu.make_async_copy(cross_end_in, cross_s.at[half:], in_sem.at[1])
        carry_own.start()
        carry_end.start()
        far = feature_block(z, 2, 1) ^ p
        pltpu.make_async_copy(rows.source(row_refs, 2, 1, width), rows_s.at[2], row_sem.at[2]).start()
        own.start_any(own_refs, far, own_s, own_sem)
        for i in range(2):
            f = p ^ (6 + i)
            for zbits in range(4):
                for side in range(2):
                    @pl.when((z ^ (f // 2) == zbits) & (f % 2 == side))
                    def _():
                        source = rows.source(row_refs, zbits, side, width)
                        pltpu.make_async_copy(source, rows_s.at[i], row_sem.at[i]).start()
            end.start(end_refs, 6 + i, end_s.at[i], end_sem.at[i])

        @pl.when(far < 6)
        def _():
            end.start_any(end_refs, far, end_s.at[2], end_sem.at[2])

        carry_own.wait()
        wait(rows_s.at[2], row_sem.at[2])
        wait(own_s, own_sem)
        tiled_product(cross_s.at[:half], rows_s.at[2], own_s)
        row_norm_s[...] = row_norm_in[...]
        add_squares(row_norm_s, rows_s.at[2])
        carry_end.wait()
        for i in range(2):
            wait(rows_s.at[i], row_sem.at[i])
            wait(end_s.at[i], end_sem.at[i])
            tiled_product(cross_s.at[half:], rows_s.at[i], end_s.at[i])
            add_squares(norm_s, end_s.at[i], first=i == 0)

        @pl.when(far < 6)
        def _():
            wait(end_s.at[2], end_sem.at[2])
            tiled_product(cross_s.at[half:], rows_s.at[2], end_s.at[2])

        row_norm = jnp.sum(row_norm_s[...], axis=1, keepdims=True)
        for t in range(2 * half):
            inside = slice(t * 256, (t + 1) * 256)
            if t < half:
                norm = norm_own_in[:1, inside]
            else:
                here = slice((t - half) * 256, (t - half + 1) * 256)
                norm = norm_end_in[:1, here] + across_lanes(norm_s, here)[:1]
            k = jnp.exp(-(row_norm + norm - 2.0 * cross_s[t]) / SPREAD)
            kernel_ref[:, inside] = k
            sums_s[:count, inside] = jnp.dot(columns_ref[...], k, precision=lax.Precision.HIGHEST)
            sums_s[count:, inside] = jnp.broadcast_to(jnp.sum(k * k, axis=0, keepdims=True), (8, 256))
        odd = p % 2 == 1
        mine_ref[...] = jnp.where(odd, sums_s[:, m:], sums_s[:, :m])
        other_ref[...] = jnp.where(odd, sums_s[:, :m], sums_s[:, m:])

    return call(
        body,
        [place(), cross_own, cross_end, row_norm, norm_own, norm_end, columns]
        + rows.blocks + own.blocks + end.blocks,
        [SMEM] + [ANY] * 2 + [VMEM] * 4 + [ANY] * (len(rows.keys) + len(own.keys) + len(end.keys)),
        [(n, 2 * m), (count + 8, m), (count + 8, m)],
        [
            pltpu.VMEM((2 * m // 256, n, 256), jnp.float32),
            pltpu.VMEM((3, n, width), jnp.bfloat16),
            pltpu.VMEM((m, width), jnp.bfloat16),
            pltpu.VMEM((3, m, width), jnp.bfloat16),
            pltpu.VMEM((n, 128), jnp.float32),
            pltpu.VMEM((m, 128), jnp.float32),
            pltpu.VMEM((count + 8, 2 * m), jnp.float32),
            pltpu.SemaphoreType.DMA((3,)),
            pltpu.SemaphoreType.DMA,
            pltpu.SemaphoreType.DMA((3,)),
            pltpu.SemaphoreType.DMA((2,)),
        ],
        "last_block",
    )


def middle_kernel(row_features, landmark_features, columns):
    own = landmark_features
    m, half = own.shape
    n, middle = row_features.shape[0], m // 2
    left, right = row_features[:, :half], row_features[:, half:]
    end = handed(own)
    own_x, own_y = flipped(own, 2), flipped(own, 4)
    middle_rows = across(row_features)
    own_x, own_y, end, left = lax.optimization_barrier((own_x, own_y, end, left))
    end_left = handed(left)
    own_low, own_high = flipped(own_x[:middle], 4), flipped(own_y[middle:], 2)
    other_own, other_x, other_y = flipped(after(own, own_x), 1), flipped(own_x, 1), flipped(own_y, 1)
    own_low, own_high, end = lax.optimization_barrier((own_low, own_high, end))
    end_x, end_y = flipped(end, 2), flipped(end, 4)
    other_low, other_high = flipped(own_low, 1), flipped(own_high, 1)
    end_bottom = end[middle:]
    end_left, right, middle_rows = lax.optimization_barrier((end_left, right, middle_rows))
    far_left = across(end_left)
    end_right = handed(right)
    own_parts = [
        (0, 0, own), (2, 0, own_x), (4, 0, own_y), (6, 0, own_low), (6, middle, own_high),
        (1, 0, other_own), (3, 0, other_x), (5, 0, other_y), (7, 0, other_low), (7, middle, other_high),
    ]
    rows = {(0, None): row_features, (3, None): middle_rows, (1, 0): end_left}
    cross_own, row_norm, norm_own = own_block(rows, own_parts, n, m, half)
    end_x, end_y, end_bottom, far_left, _ = lax.optimization_barrier((end_x, end_y, end_bottom, far_left, cross_own))
    end_high = flipped(end_bottom, 6)
    end_right = after(end_right, end_x, end_y)
    far_right = across(end_right)
    end_low = handed(after(own_low, end_right))
    end_parts = [(0, 0, end), (2, 0, end_x), (4, 0, end_y)]
    end_parts += [(bits + 1, row, flipped(block, 1)) for bits, row, block in end_parts]
    rows |= {(1, 1): end_right, (2, 0): far_left}
    cross_own, cross_end, row_norm, norm_end = end_block(
        rows, own_parts, end_parts, cross_own, row_norm, n, m, half
    )
    corner = [(6, 0, after(end_low, cross_end)), (6, middle, after(end_high, cross_end, far_right))]
    end_parts += corner + [(bits + 1, row, flipped(block, 1)) for bits, row, block in corner]
    rows |= {(2, 1): far_right}
    return last_block(
        rows, own_parts, end_parts, cross_own, cross_end, row_norm, norm_own, norm_end, columns, half
    )


def conjugate_gradients(kernel, sums, columns, lam, sum_rows, sum_landmarks, settle=None):
    count = columns.shape[0]
    residual, precond = sums[:count], lam + sums[count]
    coefficient = jnp.zeros_like(residual)
    inner = None
    for iteration in range(ITERS):
        scaled = residual / precond
        part = times(scaled, kernel, (1, 1))
        dots = [jnp.sum(residual * scaled, axis=1), jnp.sum(scaled * scaled, axis=1)]
        if iteration > 0:
            dots.append(jnp.sum(scaled * direction, axis=1))
        sums = sum_landmarks(packed(part, *dots))
        inner_next, square = sums[count, :count], sums[count + 1, :count]
        if iteration == 0:
            direction, image, length = scaled, sums[:count], square
        else:
            beta = inner_next / inner
            length = square + beta * (2.0 * sums[count + 2, :count] + beta * length)
            direction = scaled + beta[:, None] * direction
            image = sums[:count] + beta[:, None] * image
        inner = inner_next
        last = packed(times(image, kernel, (1, 0)), jnp.sum(image * image, axis=1))
        if settle is not None and iteration == ITERS - 1:
            state, finish = settle((coefficient, residual, direction), packed_twice((inner, lam * length), last.shape[1]))
            sums = finish(last.at[count:].set(packed_twice((jnp.sum(image * image, axis=1),), last.shape[1])))
            coefficient, residual, direction = (state[i * count : (i + 1) * count] for i in range(3))
            inner, ridge = state[3 * count, :count], state[3 * count + 1, :count]
        else:
            sums = sum_rows(last)
            ridge = lam * length
        gradient = sums[:count] + lam * direction
        step_size = (inner / (sums[count, :count] + ridge))[:, None]
        coefficient = coefficient + step_size * direction
        residual = residual - step_size * gradient
    return coefficient, residual


def packed_twice(vectors, width):
    rows = jnp.stack(vectors)
    rows = jnp.pad(rows, ((0, 8 - rows.shape[0]), (0, width // 2 - rows.shape[1])))
    return jnp.concatenate([rows, rows], axis=1)


def settled(state, vectors):
    z = lax.axis_index("landmark")
    middle = (z == 1) | (z == 2)
    odd = lax.axis_index("proof") % 2 == 1
    half = vectors.shape[1] // 2

    def taken(*blocks):
        whole = jnp.concatenate(blocks, axis=0)
        return jnp.where(middle, whole[:, :half], handed(whole[:, half:]))

    def finish(block):
        low, high, end_low, end_high = (block[:, i * half // 2 : (i + 1) * half // 2] for i in range(4))
        mine, other = jnp.where(odd, high, low), jnp.where(odd, low, high)
        end_mine, end_other = jnp.where(odd, end_high, end_low), jnp.where(odd, end_low, end_high)
        both = jnp.concatenate([mine, end_mine], axis=1) + flipped(jnp.concatenate([other, end_other], axis=1), 1)
        work = jnp.where(middle, both[:, : half // 2], handed(both[:, half // 2 :]))
        work = work + flipped(work, 2) + flipped(work, 4) + flipped(work, 6)
        other = flipped(work, 1)
        return jnp.concatenate([jnp.where(odd, other, work), jnp.where(odd, work, other)], axis=1)

    return jnp.concatenate([taken(*state[:2]), taken(state[2], vectors)], axis=0), finish


def folded(row_features, landmark_features, targets):
    lam = ridge_scale * row_features.shape[0] * lax.axis_size("proof")
    columns = targets.T
    kernel, mine, other = middle_kernel(row_features, landmark_features, columns)
    sums = sum_halves(mine, other)
    coefficient, residual = conjugate_gradients(kernel, sums, columns, lam, sum_rows_axis, sum_middle, settled)
    return coefficient.T, residual.T


def plain(row_features, landmark_features, targets):
    lam = ridge_scale * row_features.shape[0] * lax.axis_size("proof")
    columns = targets.T
    rows = lax.all_gather(row_features, "landmark", axis=1, tiled=True)
    whole = lax.all_gather(landmark_features, "proof", axis=1, tiled=True)
    kernel = jnp.exp(-(squares(rows)[:, None] + squares(whole)[None, :] - 2.0 * cross_piece(rows, whole)) / SPREAD)
    sum_rows = lambda block: lax.psum(block, "proof")
    sums = sum_rows(packed(times(columns, kernel, (1, 0)), jnp.sum(kernel * kernel, axis=0)))
    sum_landmarks = lambda block: lax.psum(block, "landmark")
    coefficient, residual = conjugate_gradients(kernel, sums, columns, lam, sum_rows, sum_landmarks)
    return coefficient.T, residual.T


def solution(mesh):
    placed = (P("proof", "landmark"), P("landmark", "proof"), P("proof", None))
    four_planes = mesh.shape["proof"] == 8 and mesh.shape["landmark"] == 4
    return jax.shard_map(
        folded if four_planes else plain,
        mesh=mesh,
        in_specs=placed,
        out_specs=(P("landmark", None), P("landmark", None)),
        check_vma=False,
    )
```

```python
import jax
import jax.numpy as jnp
from jax import lax
from jax.experimental import pallas as pl
from jax.experimental.pallas import tpu as pltpu
from jax.sharding import PartitionSpec as P

ITERS = 2
SPREAD = 10690

ridge_scale = 0.002


def squares(block):
    return jnp.sum(jnp.square(block.astype(jnp.float32)), axis=1)


def cross_piece(left, right):
    return lax.dot_general(
        left, right, (((1,), (1,)), ((), ())), preferred_element_type=jnp.float32
    )


def times(left, right, contract):
    return lax.dot_general(
        left, right, ((contract[:1], contract[1:]), ((), ())), precision=lax.Precision.HIGHEST
    )


NEIGHBOURS = [(0, 1), (1, 0), (2, 3), (3, 2)]


def handed(block):
    return lax.ppermute(block, "landmark", NEIGHBOURS)


def across(block):
    pairs = [(4 * p + z, 4 * p + 3 - z if z in (1, 2) else 4 * (p ^ 1) + z) for p in range(8) for z in range(4)]
    return lax.ppermute(block, ("proof", "landmark"), pairs)


def flipped(block, bits):
    return lax.ppermute(block, "proof", [(i, i ^ bits) for i in range(8)])


def sum_rows_axis(block):
    odd = lax.axis_index("proof") % 2
    half = block.shape[1] // 2
    low, high = block[:, :half], block[:, half:]
    return sum_halves(jnp.where(odd == 0, low, high), jnp.where(odd == 0, high, low))


def sum_halves(mine, other):
    odd = lax.axis_index("proof") % 2
    mine = mine + flipped(other, 1)
    mine = mine + flipped(mine, 2) + flipped(mine, 4) + flipped(mine, 6)
    other = flipped(mine, 1)
    low, high = jnp.where(odd == 0, mine, other), jnp.where(odd == 0, other, mine)
    return jnp.concatenate([low, high], axis=1)


def sum_middle(block):
    return block + across(block)


def packed(block, *vectors):
    rows = jnp.stack(vectors)
    rows = jnp.pad(rows, ((0, 8 - rows.shape[0]), (0, block.shape[1] - rows.shape[1])))
    return jnp.concatenate([block, rows], axis=0)


def after(block, *earlier):
    return lax.optimization_barrier((block, *earlier))[0]


ANY = pl.BlockSpec(memory_space=pltpu.HBM)
VMEM = pl.BlockSpec(memory_space=pltpu.VMEM)
SMEM = pl.BlockSpec(memory_space=pltpu.SMEM)


def place():
    return jnp.stack([lax.axis_index("proof"), lax.axis_index("landmark")]).astype(jnp.int32)


def add_squares(total_ref, block_ref, first=False):
    for r in range(0, block_ref.shape[0], 32):
        rows = slice(r, r + 32)
        total = None if first else total_ref[rows]
        for j in range(block_ref.shape[1] // 128):
            x = block_ref[rows, j * 128 : (j + 1) * 128].astype(jnp.float32)
            total = x * x if total is None else total + x * x
        total_ref[rows] = total


def across_lanes(norm_ref, inside):
    ones = jnp.ones((8, 128), jnp.float32)
    return lax.dot_general(ones, norm_ref[inside], (((1,), (1,)), ((), ())), precision=lax.Precision.HIGHEST)


def product(left, right):
    return lax.dot_general(left, right, (((1,), (1,)), ((), ())), preferred_element_type=jnp.float32)


def tiled_product(cross_ref, left, right_ref):
    for t in range(cross_ref.shape[0]):
        cross_ref[t] += product(left[...], right_ref[t * 256 : (t + 1) * 256])


def feature_block(z, zbits, side):
    return 2 * (z ^ zbits) + side


class Rows:
    def __init__(self, blocks):
        self.keys, self.blocks = list(blocks), list(blocks.values())

    def source(self, refs, zbits, side, width):
        if (zbits, None) in self.keys:
            return refs[self.keys.index((zbits, None))].at[:, pl.ds(side * width, width)]
        return refs[self.keys.index((zbits, side))]


class Landmarks:
    def __init__(self, parts):
        self.keys = [(bits, row) for bits, row, _ in parts]
        self.blocks = [block for _, _, block in parts]

    def start(self, refs, bits, target, sem):
        for (found, row), ref in zip(self.keys, refs):
            if found == bits:
                pltpu.make_async_copy(ref, target.at[pl.ds(row, ref.shape[0])], sem).start()

    def start_any(self, refs, bits, target, sem):
        for one in sorted({found for found, _ in self.keys}):
            @pl.when(bits == one)
            def _():
                self.start(refs, one, target, sem)


def wait(target, sem):
    pltpu.make_async_copy(target, target, sem).wait()


def call(body, inputs, specs, shapes, scratch, name):
    return pl.pallas_call(
        body,
        out_shape=tuple(jax.ShapeDtypeStruct(shape, jnp.float32) for shape in shapes),
        in_specs=specs,
        out_specs=tuple(VMEM for _ in shapes),
        scratch_shapes=scratch,
        compiler_params=pltpu.CompilerParams(vmem_limit_bytes=60 << 20),
        cost_estimate=pl.CostEstimate(flops=1000, bytes_accessed=1000, transcendentals=0),
        name=name,
    )(*inputs)


def own_block(rows, landmarks, n, m, width):
    rows, landmarks = Rows(rows), Landmarks(landmarks)
    sources = [(0, 0), (0, 1), (3, 0), (3, 1), (1, 0)]

    def body(place_ref, *refs):
        row_refs, refs = refs[: len(rows.keys)], refs[len(rows.keys) :]
        landmark_refs, refs = refs[: len(landmarks.keys)], refs[len(landmarks.keys) :]
        cross_ref, row_norm_ref, norm_ref, rows_s, land_s, norm_s, row_sem, land_sem = refs
        p, z = place_ref[0], place_ref[1]
        wanted = [feature_block(z, zbits, side) ^ p for zbits, side in sources]
        for i, (zbits, side) in enumerate(sources):
            pltpu.make_async_copy(rows.source(row_refs, zbits, side, width), rows_s.at[i], row_sem.at[i]).start()
        for bits in range(8):
            landmarks.start(landmark_refs, bits, land_s.at[bits], land_sem.at[bits])
        cross_ref[...] = jnp.zeros_like(cross_ref)
        for bits in range(8):
            wait(land_s.at[bits], land_sem.at[bits])
        for i in range(len(sources)):
            wait(rows_s.at[i], row_sem.at[i])
            tiled_product(cross_ref, rows_s.at[i], land_s.at[wanted[i]])
            add_squares(row_norm_ref, rows_s.at[i], first=i == 0)
            for bits in (2 * i, 2 * i + 1):
                if bits < 8:
                    add_squares(norm_s, land_s.at[bits], first=bits == 0)
        norm_ref[...] = across_lanes(norm_s, slice(None))

    return call(
        body,
        [place()] + rows.blocks + landmarks.blocks,
        [SMEM] + [ANY] * (len(rows.keys) + len(landmarks.keys)),
        [(m // 256, n, 256), (n, 128), (8, m)],
        [
            pltpu.VMEM((len(sources), n, width), jnp.bfloat16),
            pltpu.VMEM((8, m, width), jnp.bfloat16),
            pltpu.VMEM((m, 128), jnp.float32),
            pltpu.SemaphoreType.DMA((len(sources),)),
            pltpu.SemaphoreType.DMA((8,)),
        ],
        "own_block",
    )


def end_block(rows, own, end, cross_own, row_norm, n, m, width):
    rows, own, end = Rows(rows), Landmarks(own), Landmarks(end)
    late = 2 * 2 + 1

    def body(place_ref, cross_in, norm_in, *refs):
        row_refs, refs = refs[: len(rows.keys)], refs[len(rows.keys) :]
        own_refs, refs = refs[: len(own.keys)], refs[len(own.keys) :]
        end_refs, refs = refs[: len(end.keys)], refs[len(end.keys) :]
        cross_own_ref, cross_ref, row_norm_ref, norm_ref, rows_s, own_s, end_s, norm_s, row_sem, own_sem, end_sem, in_sem = refs
        p, z = place_ref[0], place_ref[1]
        more = [(1, 1), (2, 0)]
        carry = pltpu.make_async_copy(cross_in, cross_own_ref, in_sem)
        carry.start()
        for zbits, side in more:
            slot = 2 * zbits + side
            pltpu.make_async_copy(rows.source(row_refs, zbits, side, width), rows_s.at[slot], row_sem.at[slot]).start()
        for i, (zbits, side) in enumerate(more):
            own.start_any(own_refs, feature_block(z, zbits, side) ^ p, own_s.at[i], own_sem.at[i])
        for slot in range(8):
            if slot != late and (slot // 2, slot % 2) not in more:
                source = rows.source(row_refs, slot // 2, slot % 2, width)
                pltpu.make_async_copy(source, rows_s.at[slot], row_sem.at[slot]).start()
        for bits in range(6):
            end.start(end_refs, bits, end_s.at[bits], end_sem.at[bits])
        cross_ref[...] = jnp.zeros_like(cross_ref)
        rows_s[late] = jnp.zeros(rows_s.shape[1:], rows_s.dtype)
        row_norm_ref[...] = norm_in[...]
        carry.wait()
        for i, (zbits, side) in enumerate(more):
            slot = 2 * zbits + side
            wait(rows_s.at[slot], row_sem.at[slot])
            wait(own_s.at[i], own_sem.at[i])
            tiled_product(cross_own_ref, rows_s.at[slot], own_s.at[i])
            add_squares(row_norm_ref, rows_s.at[slot])
        for slot in range(8):
            if slot != late and (slot // 2, slot % 2) not in more:
                wait(rows_s.at[slot], row_sem.at[slot])
        for bits in range(6):
            wait(end_s.at[bits], end_sem.at[bits])
            f = p ^ bits
            slot = 2 * (z ^ (f // 2)) + f % 2
            tiled_product(cross_ref, rows_s.at[slot], end_s.at[bits])
            add_squares(norm_s, end_s.at[bits], first=bits == 0)
        norm_ref[...] = across_lanes(norm_s, slice(None))

    return call(
        body,
        [place(), cross_own, row_norm] + rows.blocks + own.blocks + end.blocks,
        [SMEM, ANY, VMEM] + [ANY] * (len(rows.keys) + len(own.keys) + len(end.keys)),
        [(m // 256, n, 256), (m // 256, n, 256), (n, 128), (8, m)],
        [
            pltpu.VMEM((8, n, width), jnp.bfloat16),
            pltpu.VMEM((2, m, width), jnp.bfloat16),
            pltpu.VMEM((6, m, width), jnp.bfloat16),
            pltpu.VMEM((m, 128), jnp.float32),
            pltpu.SemaphoreType.DMA((8,)),
            pltpu.SemaphoreType.DMA((2,)),
            pltpu.SemaphoreType.DMA((6,)),
            pltpu.SemaphoreType.DMA,
        ],
        "end_block",
    )


def last_block(rows, own, end, cross_own, cross_end, row_norm, norm_own, norm_end, columns, width):
    rows, own, end = Rows(rows), Landmarks(own), Landmarks(end)
    n, m, count = columns.shape[1], norm_own.shape[1], columns.shape[0]

    def body(place_ref, cross_own_in, cross_end_in, row_norm_in, norm_own_in, norm_end_in, columns_ref, *refs):
        row_refs, refs = refs[: len(rows.keys)], refs[len(rows.keys) :]
        own_refs, refs = refs[: len(own.keys)], refs[len(own.keys) :]
        end_refs, refs = refs[: len(end.keys)], refs[len(end.keys) :]
        kernel_ref, mine_ref, other_ref, *refs = refs
        cross_s, rows_s, own_s, end_s, row_norm_s, norm_s, sums_s, row_sem, own_sem, end_sem, in_sem = refs
        p, z = place_ref[0], place_ref[1]
        half = m // 256
        carry_own = pltpu.make_async_copy(cross_own_in, cross_s.at[:half], in_sem.at[0])
        carry_end = pltpu.make_async_copy(cross_end_in, cross_s.at[half:], in_sem.at[1])
        carry_own.start()
        carry_end.start()
        far = feature_block(z, 2, 1) ^ p
        pltpu.make_async_copy(rows.source(row_refs, 2, 1, width), rows_s.at[2], row_sem.at[2]).start()
        own.start_any(own_refs, far, own_s, own_sem)
        for i in range(2):
            f = p ^ (6 + i)
            for zbits in range(4):
                for side in range(2):
                    @pl.when((z ^ (f // 2) == zbits) & (f % 2 == side))
                    def _():
                        source = rows.source(row_refs, zbits, side, width)
                        pltpu.make_async_copy(source, rows_s.at[i], row_sem.at[i]).start()
            end.start(end_refs, 6 + i, end_s.at[i], end_sem.at[i])

        @pl.when(far < 6)
        def _():
            end.start_any(end_refs, far, end_s.at[2], end_sem.at[2])

        carry_own.wait()
        wait(rows_s.at[2], row_sem.at[2])
        wait(own_s, own_sem)
        tiled_product(cross_s.at[:half], rows_s.at[2], own_s)
        row_norm_s[...] = row_norm_in[...]
        add_squares(row_norm_s, rows_s.at[2])
        carry_end.wait()
        for i in range(2):
            wait(rows_s.at[i], row_sem.at[i])
            wait(end_s.at[i], end_sem.at[i])
            tiled_product(cross_s.at[half:], rows_s.at[i], end_s.at[i])
            add_squares(norm_s, end_s.at[i], first=i == 0)

        @pl.when(far < 6)
        def _():
            wait(end_s.at[2], end_sem.at[2])
            tiled_product(cross_s.at[half:], rows_s.at[2], end_s.at[2])

        row_norm = jnp.sum(row_norm_s[...], axis=1, keepdims=True)
        for t in range(2 * half):
            inside = slice(t * 256, (t + 1) * 256)
            if t < half:
                norm = norm_own_in[:1, inside]
            else:
                here = slice((t - half) * 256, (t - half + 1) * 256)
                norm = norm_end_in[:1, here] + across_lanes(norm_s, here)[:1]
            k = jnp.exp(-(row_norm + norm - 2.0 * cross_s[t]) / SPREAD)
            kernel_ref[:, inside] = k
            sums_s[:count, inside] = jnp.dot(columns_ref[...], k, precision=lax.Precision.HIGHEST)
            sums_s[count:, inside] = jnp.broadcast_to(jnp.sum(k * k, axis=0, keepdims=True), (8, 256))
        odd = p % 2 == 1
        mine_ref[...] = jnp.where(odd, sums_s[:, m:], sums_s[:, :m])
        other_ref[...] = jnp.where(odd, sums_s[:, :m], sums_s[:, m:])

    return call(
        body,
        [place(), cross_own, cross_end, row_norm, norm_own, norm_end, columns]
        + rows.blocks + own.blocks + end.blocks,
        [SMEM] + [ANY] * 2 + [VMEM] * 4 + [ANY] * (len(rows.keys) + len(own.keys) + len(end.keys)),
        [(n, 2 * m), (count + 8, m), (count + 8, m)],
        [
            pltpu.VMEM((2 * m // 256, n, 256), jnp.float32),
            pltpu.VMEM((3, n, width), jnp.bfloat16),
            pltpu.VMEM((m, width), jnp.bfloat16),
            pltpu.VMEM((3, m, width), jnp.bfloat16),
            pltpu.VMEM((n, 128), jnp.float32),
            pltpu.VMEM((m, 128), jnp.float32),
            pltpu.VMEM((count + 8, 2 * m), jnp.float32),
            pltpu.SemaphoreType.DMA((3,)),
            pltpu.SemaphoreType.DMA,
            pltpu.SemaphoreType.DMA((3,)),
            pltpu.SemaphoreType.DMA((2,)),
        ],
        "last_block",
    )


def middle_kernel(row_features, landmark_features, columns):
    own = landmark_features
    m, half = own.shape
    n, middle = row_features.shape[0], m // 2
    left, right = row_features[:, :half], row_features[:, half:]
    end = handed(own)
    own_x, own_y = flipped(own, 2), flipped(own, 4)
    middle_rows = across(row_features)
    end_left = handed(after(left, end))
    own_x, own_y = lax.optimization_barrier((own_x, own_y))
    own_low, own_high = flipped(own_x[:middle], 4), flipped(own_y[middle:], 2)
    other_own, other_x, other_y = flipped(after(own, own_x), 1), flipped(own_x, 1), flipped(own_y, 1)
    own_low, own_high, end = lax.optimization_barrier((own_low, own_high, end))
    end_x, end_y = flipped(end, 2), flipped(end, 4)
    other_low, other_high = flipped(own_low, 1), flipped(own_high, 1)
    end_bottom = end[middle:]
    end_left, right, middle_rows = lax.optimization_barrier((end_left, right, middle_rows))
    far_left = across(end_left)
    end_right = handed(right)
    own_parts = [
        (0, 0, own), (2, 0, own_x), (4, 0, own_y), (6, 0, own_low), (6, middle, own_high),
        (1, 0, other_own), (3, 0, other_x), (5, 0, other_y), (7, 0, other_low), (7, middle, other_high),
    ]
    rows = {(0, None): row_features, (3, None): middle_rows, (1, 0): end_left}
    cross_own, row_norm, norm_own = own_block(rows, own_parts, n, m, half)
    end_x, end_y, end_bottom, far_left, _ = lax.optimization_barrier((end_x, end_y, end_bottom, far_left, cross_own))
    end_high = flipped(end_bottom, 6)
    end_right = after(end_right, cross_own)
    far_right = across(end_right)
    end_low = handed(after(own_low, end_right, end_x, end_y))
    end_parts = [(0, 0, end), (2, 0, end_x), (4, 0, end_y)]
    end_parts += [(bits + 1, row, flipped(block, 1)) for bits, row, block in end_parts]
    rows |= {(1, 1): end_right, (2, 0): far_left}
    cross_own, cross_end, row_norm, norm_end = end_block(
        rows, own_parts, end_parts, cross_own, row_norm, n, m, half
    )
    corner = [(6, 0, after(end_low, cross_end)), (6, middle, after(end_high, cross_end, far_right))]
    end_parts += corner + [(bits + 1, row, flipped(block, 1)) for bits, row, block in corner]
    rows |= {(2, 1): far_right}
    return last_block(
        rows, own_parts, end_parts, cross_own, cross_end, row_norm, norm_own, norm_end, columns, half
    )


def conjugate_gradients(kernel, sums, columns, lam, sum_rows, sum_landmarks, settle=None):
    count = columns.shape[0]
    residual, precond = sums[:count], lam + sums[count]
    coefficient = jnp.zeros_like(residual)
    inner = None
    for iteration in range(ITERS):
        scaled = residual / precond
        part = times(scaled, kernel, (1, 1))
        dots = [jnp.sum(residual * scaled, axis=1), jnp.sum(scaled * scaled, axis=1)]
        if iteration > 0:
            dots.append(jnp.sum(scaled * direction, axis=1))
        sums = sum_landmarks(packed(part, *dots))
        inner_next, square = sums[count, :count], sums[count + 1, :count]
        if iteration == 0:
            direction, image, length = scaled, sums[:count], square
        else:
            beta = inner_next / inner
            length = square + beta * (2.0 * sums[count + 2, :count] + beta * length)
            direction = scaled + beta[:, None] * direction
            image = sums[:count] + beta[:, None] * image
        inner = inner_next
        last = packed(times(image, kernel, (1, 0)), jnp.sum(image * image, axis=1))
        if settle is not None and iteration == ITERS - 1:
            state, finish = settle((coefficient, residual, direction), packed_twice((inner, lam * length), last.shape[1]))
            sums = finish(last.at[count:].set(packed_twice((jnp.sum(image * image, axis=1),), last.shape[1])))
            coefficient, residual, direction = (state[i * count : (i + 1) * count] for i in range(3))
            inner, ridge = state[3 * count, :count], state[3 * count + 1, :count]
        else:
            sums = sum_rows(last)
            ridge = lam * length
        gradient = sums[:count] + lam * direction
        step_size = (inner / (sums[count, :count] + ridge))[:, None]
        coefficient = coefficient + step_size * direction
        residual = residual - step_size * gradient
    return coefficient, residual


def packed_twice(vectors, width):
    rows = jnp.stack(vectors)
    rows = jnp.pad(rows, ((0, 8 - rows.shape[0]), (0, width // 2 - rows.shape[1])))
    return jnp.concatenate([rows, rows], axis=1)


def settled(state, vectors):
    z = lax.axis_index("landmark")
    middle = (z == 1) | (z == 2)
    odd = lax.axis_index("proof") % 2 == 1
    half = vectors.shape[1] // 2

    def taken(*blocks):
        whole = jnp.concatenate(blocks, axis=0)
        return jnp.where(middle, whole[:, :half], handed(whole[:, half:]))

    def finish(block):
        low, high, end_low, end_high = (block[:, i * half // 2 : (i + 1) * half // 2] for i in range(4))
        mine, other = jnp.where(odd, high, low), jnp.where(odd, low, high)
        end_mine, end_other = jnp.where(odd, end_high, end_low), jnp.where(odd, end_low, end_high)
        both = jnp.concatenate([mine, end_mine], axis=1) + flipped(jnp.concatenate([other, end_other], axis=1), 1)
        work = jnp.where(middle, both[:, : half // 2], handed(both[:, half // 2 :]))
        work = work + flipped(work, 2) + flipped(work, 4) + flipped(work, 6)
        other = flipped(work, 1)
        return jnp.concatenate([jnp.where(odd, other, work), jnp.where(odd, work, other)], axis=1)

    return jnp.concatenate([taken(*state[:2]), taken(state[2], vectors)], axis=0), finish


def folded(row_features, landmark_features, targets):
    lam = ridge_scale * row_features.shape[0] * lax.axis_size("proof")
    columns = targets.T
    kernel, mine, other = middle_kernel(row_features, landmark_features, columns)
    sums = sum_halves(mine, other)
    coefficient, residual = conjugate_gradients(kernel, sums, columns, lam, sum_rows_axis, sum_middle, settled)
    return coefficient.T, residual.T


def plain(row_features, landmark_features, targets):
    lam = ridge_scale * row_features.shape[0] * lax.axis_size("proof")
    columns = targets.T
    rows = lax.all_gather(row_features, "landmark", axis=1, tiled=True)
    whole = lax.all_gather(landmark_features, "proof", axis=1, tiled=True)
    kernel = jnp.exp(-(squares(rows)[:, None] + squares(whole)[None, :] - 2.0 * cross_piece(rows, whole)) / SPREAD)
    sum_rows = lambda block: lax.psum(block, "proof")
    sums = sum_rows(packed(times(columns, kernel, (1, 0)), jnp.sum(kernel * kernel, axis=0)))
    sum_landmarks = lambda block: lax.psum(block, "landmark")
    coefficient, residual = conjugate_gradients(kernel, sums, columns, lam, sum_rows, sum_landmarks)
    return coefficient.T, residual.T


def solution(mesh):
    placed = (P("proof", "landmark"), P("landmark", "proof"), P("proof", None))
    four_planes = mesh.shape["proof"] == 8 and mesh.shape["landmark"] == 4
    return jax.shard_map(
        folded if four_planes else plain,
        mesh=mesh,
        in_specs=placed,
        out_specs=(P("landmark", None), P("landmark", None)),
        check_vma=False,
    )
```
